128 devices in a mesh: grp: 4 (over x), gx: 4 (over z_lo, core), gy: 8 (over z_hi, y).
Axes of the slice: x: 4, y: 4, z: 4 (z_hi: 2, z_lo: 2; z = z_hi * 2 + z_lo), core: 2. Of those that a mesh axis runs over, the one named last changes fastest.
Arguments:
- flow_state: float32 [8, 768, 128, 128], P(None, ('grp', 'gx'), 'gy'), may hold values from -90 to 90
- speeds: float32 [3, 8], replicated, may hold values from 0.3 to 1.2
- viscosity: float32 [8], replicated, may hold values from 0.02 to 0.2
- reaction: float32 [8, 8], replicated, may hold values from -2 to 2
- start_basis: float32 [768, 96], replicated, may hold values from -6 to 6
- slab_table: int32 [8, 8, 1], replicated, may hold values from 0 to 15; in each aligned block of 8 rows (0 to 7, 8 to 15, ..., all dimensions but the last counted through in order) at most 2 rows name the same one
Outputs:
- final_state: float32 [8, 768, 128, 128], P(None, ('grp', 'gx'), 'gy')
- core_slots: float32 [256, 96, 8, 2, 128], P(('grp', 'gx', 'gy'))
The draws below stay inside these ranges and needn't reach their ends.
Inputs may be any that keep to these rules, and one draw needn't show every extreme that they name: slab_table[t, u, 0] names the slab that stores unit u of row t; within each row t no slab is named by more than 2 units, a bound that some block reaches.
All inputs are finite; a program needn't handle non-finite values.
Results may differ from the reference program's by a relative error of at most 0.0034.
Values may be sent and summed in bfloat16 or wider, within the bound.
A program may use at most 256 MiB of HBM per device.

```python
import math
import jax
import jax.numpy as jnp
import numpy as np
from jax import lax

V = 8
NX = 768
R = 96
NZ = 128
YB = 2
NEWTON = 5
NY = 128
UNITS = 8
SLABS = 16
MOST = 2
SLOTS = 256
N_GY = 8


def draw_flow_state(key, part):
    key_noise = jax.random.fold_in(key, 11)
    key_scale = jax.random.fold_in(key, 23)
    rising = 1.0 + 2.0 * jnp.arange(NY, dtype=jnp.float32) / NY
    noise_field = jax.random.truncated_normal(key_noise, -4.0, 4.0, (V, NX, NY, NZ), jnp.float32)
    scales = jnp.exp(jax.random.uniform(key_scale, (NX, NY), jnp.float32, math.log(0.3), math.log(3.0)))
    blended = noise_field + 0.8 * jnp.roll(noise_field, 1, axis=1)
    return (blended * (scales * rising[None, :])[None, :, :, None]).astype(jnp.float32)


def assign_block(key, own, number, rows, count, top, most, skew):
    ranking = jax.random.permutation(key, count)
    packed, usual = load_shares(count, rows * top, most, skew, True), load_shares(count, rows * top, most, skew, False)
    places = jnp.arange(count)

    def named(tallies, rotation):
        used = int((tallies > 0).sum())
        fixed = max(1, used // 4)
        passed = fixed + (places - fixed + rotation * (used - fixed)) % max(1, count - fixed)
        return jnp.zeros((count,), jnp.int32).at[ranking[jnp.where(places < fixed, places, passed)]].set(jnp.asarray(tallies, jnp.int32))

    tallies = jnp.where(number % 4 == 0, named(packed, number // 4), named(usual, number - number // 4 - 1))
    mixed = jax.random.permutation(jax.random.fold_in(own, 3), count)
    donor, receiver = mixed[0:count // 2 * 2:2], mixed[1:count // 2 * 2:2]
    margin = jnp.minimum(tallies[donor] - 1, most - tallies[receiver]) // 2
    margin = jnp.where((donor == ranking[0]) | (receiver == ranking[0]) | (tallies[receiver] == 0), 0, jnp.maximum(margin, 0))
    passed = jax.random.randint(jax.random.fold_in(own, 4), (count // 2,), 0, 1 << 20) % (margin + 1)
    tallies = tallies.at[donor].add(-passed).at[receiver].add(passed)
    items = jnp.searchsorted(jnp.cumsum(tallies), jnp.arange(rows * top), side="right").astype(jnp.int32)
    grid = items.reshape(top, rows).T
    grid = grid[jax.random.permutation(jax.random.fold_in(own, 1), rows)]
    rotation = jax.random.randint(jax.random.fold_in(own, 2), (rows, 1), 0, top)
    return jnp.take_along_axis(grid, (jnp.arange(top)[None, :] + rotation) % top, axis=1)


def load_shares(count, total, most, skew, full):
    weights = [(1 << 20) // math.isqrt(grade ** skew) + 1 for grade in range(1, count + 1)]
    largest = most if full else min(most, max(-(-total // count), total * weights[0] // sum(weights)))
    least = 1 if total - largest >= count - 1 else 0
    holding, spare = [largest] + [least] * (count - 1), total - largest - least * (count - 1)
    while spare > 0:
        candidates = [i for i in range(1, count) if holding[i] < largest] or [i for i in range(1, count) if holding[i] < most]
        pool, budget = sum([weights[i] for i in candidates]), spare
        for i in candidates:
            addition = min(most - holding[i], max(1, budget * weights[i] // pool), spare)
            holding[i] = holding[i] + addition
            spare = spare - addition
    return np.array(holding)


def scatter_about(rng, dims, width, bound, held_as=jnp.bfloat16):
    return jnp.clip(width * jax.random.normal(rng, dims, jnp.float32), -bound, bound).astype(held_as)


def setup_inputs(seed: int = 0) -> dict:
    seeds = jax.random.split(jax.random.key(seed), 7)
    flow_state = draw_flow_state(jax.random.fold_in(seeds[6], 71), 0)
    speeds = jnp.clip(jnp.exp(jax.random.uniform(seeds[1], (3, V), jnp.float32, math.log(0.3), math.log(1.2))), 0.3, 1.2)
    viscosity = jnp.clip(jnp.exp(jax.random.uniform(seeds[2], (V,), jnp.float32, math.log(0.02), math.log(0.2))), 0.02, 0.2)
    reaction = scatter_about(seeds[3], (V, V), V ** -0.5, 2.0, jnp.float32)
    start_basis = scatter_about(seeds[4], (NX, R), 1.0, 6.0, jnp.float32)
    slab_table_keys = jax.random.split(jax.random.fold_in(seeds[5], 1), N_GY * UNITS // UNITS)
    slab_table_turns = jax.random.permutation(jax.random.fold_in(seeds[5], 3), N_GY * UNITS // UNITS)
    slab_table = jax.vmap(lambda own, number: assign_block(jax.random.fold_in(seeds[5], 2), own, number, UNITS, SLABS, 1, MOST, 2))(slab_table_keys, slab_table_turns).reshape((N_GY, UNITS, 1))
    return dict(flow_state=flow_state, speeds=speeds, viscosity=viscosity, reaction=reaction, start_basis=start_basis, slab_table=slab_table)


slope_weights = (0.8, -0.2, 4.0 / 105.0, -1.0 / 280.0)
curve_weights = (1.6, -0.2, 8.0 / 315.0, -1.0 / 560.0)
curve_center = -205.0 / 72.0
time_step = 0.2

def tendency(padded, speeds, viscosity, reaction):
    center = padded[:, 4:-4, 4:-4, :]
    width_first = center.shape[1]
    width_second = center.shape[2]
    diffusion = viscosity[:, None, None, None]
    speed_one = speeds[0][:, None, None, None]
    speed_two = speeds[1][:, None, None, None]
    speed_three = speeds[2][:, None, None, None]
    summed = 3.0 * curve_center * diffusion * center
    summed = summed + jnp.einsum('kj,jxyz->kxyz', reaction, center, precision=lax.Precision.HIGHEST)
    for offset in range(1, 5):
        slope_weight = slope_weights[offset - 1]
        curve_weight = curve_weights[offset - 1]
        forward = padded[:, 4 + offset:4 + offset + width_first, 4:4 + width_second, :]
        backward = padded[:, 4 - offset:4 - offset + width_first, 4:4 + width_second, :]
        summed = summed + (curve_weight * diffusion - slope_weight * speed_one) * forward
        summed = summed + (curve_weight * diffusion + slope_weight * speed_one) * backward
        forward = padded[:, 4:4 + width_first, 4 + offset:4 + offset + width_second, :]
        backward = padded[:, 4:4 + width_first, 4 - offset:4 - offset + width_second, :]
        summed = summed + (curve_weight * diffusion - slope_weight * speed_two) * forward
        summed = summed + (curve_weight * diffusion + slope_weight * speed_two) * backward
        forward = jnp.roll(center, -offset, 3)
        backward = jnp.roll(center, offset, 3)
        summed = summed + (curve_weight * diffusion - slope_weight * speed_three) * forward
        summed = summed + (curve_weight * diffusion + slope_weight * speed_three) * backward
    return summed

def wrapped(field):
    return jnp.pad(field, ((0, 0), (4, 4), (4, 4), (0, 0)), mode='wrap')

def reference(flow_state, speeds, viscosity, reaction, start_basis, slab_table):
    first = flow_state + time_step * tendency(wrapped(flow_state), speeds, viscosity, reaction)
    final_state = 0.5 * flow_state + 0.5 * (first + time_step * tendency(wrapped(first), speeds, viscosity, reaction))
    snapshot = lax.optimization_barrier(final_state.astype(jnp.bfloat16))
    gram = jnp.zeros((NX, NX), jnp.float32)
    for variable in range(V):
        plane = snapshot[variable].astype(jnp.float32).reshape(NX, -1)
        gram = gram + jnp.dot(plane, plane.T, precision=lax.Precision.HIGHEST)
    product = jnp.dot(gram, start_basis, precision=lax.Precision.HIGHEST)
    basis = product / jnp.sqrt(jnp.sum(product * product))
    for repeat in range(NEWTON):
        inner_gram = jnp.dot(basis.T, basis, precision=lax.Precision.HIGHEST)
        basis = 1.5 * basis - 0.5 * jnp.dot(basis, inner_gram, precision=lax.Precision.HIGHEST)
    basis_half = lax.optimization_barrier(basis.astype(jnp.bfloat16)).astype(jnp.float32)
    blocks = snapshot.astype(jnp.float32).reshape(V, NX, NY // YB, YB, NZ)
    pieces = []
    for variable in range(V):
        pieces.append(jnp.einsum('xr,xuyz->uryz', basis_half, blocks[variable], precision=lax.Precision.HIGHEST))
    unit_cores = jnp.stack(pieces, axis=2)
    table = slab_table[:, :, 0]
    unit_count = table.shape[1]
    order = jnp.arange(unit_count, dtype=jnp.int32)
    earlier = order[None, :] < order[:, None]
    same_slab = table[:, :, None] == table[:, None, :]
    slot_index = lax.optimization_barrier(jnp.sum((same_slab & earlier[None, :, :]).astype(jnp.int32), axis=2))
    tile_row = jnp.arange(table.shape[0], dtype=jnp.int32)[:, None]
    position = ((table * table.shape[0] + tile_row) * MOST + slot_index).reshape(-1).astype(jnp.int32)
    core_slots = jnp.zeros((SLOTS, R, V, YB, NZ), jnp.float32).at[position].set(unit_cores)
    return (final_state, core_slots)
```

```python
import jax
import jax.numpy as jnp
from jax import lax
from jax.experimental import pallas as pl
from jax.experimental.pallas import tpu as pltpu
from jax.sharding import PartitionSpec as P

V = 8
NX = 768
R = 96
RP = 128
NZ = 128
TX = 48
TY = 16
TILES = 16
ROWS = 8
UNITS = 8
MOST = 2
NEWTON = 5
CH = 16
CHUNKS = TX // CH
CHUNK_ORDER = (0, 2, 1)
EARLY = (2, 3, 4, 5)
LATE = (0, 1, 6, 7)
UNIT_ORDER = EARLY + LATE

slope_weights = (0.8, -0.2, 4.0 / 105.0, -1.0 / 280.0)
curve_weights = (1.6, -0.2, 8.0 / 315.0, -1.0 / 560.0)
curve_center = -205.0 / 72.0
time_step = 0.2

MESH = pl.DeviceIdType.MESH
F32 = jnp.float32
BF16 = jnp.bfloat16
NT = (((1,), (1,)), ((), ()))


def split(x):
    high = x.astype(BF16)
    return high, (x - high.astype(F32)).astype(BF16)


def mm(a, b):
    return jnp.dot(a, b, preferred_element_type=F32)


def mm_nt(a, b):
    return lax.dot_general(a, b, NT, preferred_element_type=F32)


def both(a, b):

    ah, al = split(a)
    bh, bl = split(b)
    left = jnp.concatenate([ah, ah, al], axis=1)
    right = jnp.concatenate([bh, bl, bh], axis=0)
    return mm(left, right)


def iota(shape, dim):
    return lax.broadcasted_iota(jnp.int32, shape, dim)


def curve_of(distance):
    out = jnp.zeros(distance.shape, F32)
    for m in range(1, 5):
        hit = (distance == m) | (distance == -m)
        out = jnp.where(hit, time_step * curve_weights[m - 1], out)
    return out


def slope_of(distance):
    out = jnp.zeros(distance.shape, F32)
    for m in range(1, 5):
        out = jnp.where(distance == m, -time_step * slope_weights[m - 1], out)
        out = jnp.where(distance == -m, time_step * slope_weights[m - 1], out)
    return out


def kernel(
    flow_hbm, speeds, viscosity, reaction, start_ref, table,
    final_hbm, core_hbm,
    e1, e2, acc,
    ylo_out, yhi_out, ylo_in, yhi_in,
    xlo_out, xhi_out, xlo_in, xhi_in,
    sbuf, srec,
    cz, wy, wh,
    start_t, pacc, psend, prec, qrec, pfull, prod_t, blocks, csend, crec,
    picks,
    load_sem, final_sem, core_sem,
    y_send, y_recv, x_send, x_recv, s_send, s_recv, s_own,
    p_send, p_recv, q_send, q_recv, f_send, f_recv, c_send, c_recv,
):
    grp, gx, gy = (lax.axis_index(a) for a in ("grp", "gx", "gy"))
    me = grp * 4 + gx

    def tile(i):
        return (lax.div(i, 4), lax.rem(i, 4), gy)

    def row(i):
        return (grp, gx, i)

    def wrap(i, n):
        return lax.rem(i, n)

    barrier = pltpu.get_barrier_semaphore()

    @pl.loop(1, TILES)
    def _(d):
        pl.semaphore_signal(barrier, inc=1, device_id=tile(wrap(me + d, TILES)), device_id_type=MESH)

    @pl.loop(1, ROWS)
    def _(d):
        pl.semaphore_signal(barrier, inc=1, device_id=row(wrap(gy + d, ROWS)), device_id_type=MESH)

    load = pltpu.make_async_copy(flow_hbm, e1.at[:, 4 : 4 + TX], load_sem)
    load.start()

    square = (128, 128)
    turn = (iota(square, 0) - iota(square, 1)) & 127
    turn = jnp.where(turn > 64, turn - 128, turn)
    z_curve, z_slope = curve_of(turn), slope_of(turn)
    y_shape = (TY, 128)
    y_dist = (iota(y_shape, 1) & 15) - iota(y_shape, 0)
    y_var = lax.shift_right_logical(iota(y_shape, 1), 4)
    y_curve = jnp.where(y_dist == 0, time_step * 3.0 * curve_center, curve_of(y_dist))
    y_slope = slope_of(y_dist)
    h_shape = (TY, 64)
    h_col = iota(h_shape, 1)
    h_dist = (h_col & 3) - 4 + lax.shift_right_logical(h_col, 5) * 20 - iota(h_shape, 0)
    h_var = lax.shift_right_logical(h_col, 2) & 7
    h_curve, h_slope = curve_of(h_dist), slope_of(h_dist)

    @pl.loop(0, V)
    def _(k):
        v, s2, s3 = viscosity[k], speeds[1, k], speeds[2, k]
        ch, cl = split(v * z_curve + s3 * z_slope)
        cz[k] = jnp.concatenate(
            [jnp.concatenate([ch, cl], axis=1), jnp.concatenate([ch, jnp.zeros_like(cl)], axis=1)], axis=0
        )
        w = jnp.where(y_var == k, v * y_curve + s2 * y_slope, 0.0)
        for j in range(V):
            w = w + jnp.where((y_var == j) & (y_dist == 0), time_step * reaction[k, j], 0.0)
        hi, lo = split(w)
        at = pl.ds(pl.multiple_of(k * TY, TY), TY)
        at2 = pl.ds(pl.multiple_of(128 + k * TY, TY), TY)
        wy[at, :] = jnp.concatenate([hi, hi], axis=1)
        wy[at2, :] = jnp.concatenate([lo, jnp.zeros_like(lo)], axis=1)
        hi, lo = split(jnp.where(h_var == k, v * h_curve + s2 * h_slope, 0.0))
        wh[at, :] = hi
        wh[at2, :] = lo

    f_row, f_col = iota((64, 128), 0), iota((64, 128), 1)
    f_src = (lax.shift_right_logical(f_row, 2) & 7) * 16 + (f_row & 3) + lax.shift_right_logical(f_row, 5) * 12
    face = (f_src == f_col).astype(BF16)

    q_row, q_col = iota((128, 256), 0), iota((128, 256), 1)
    q_unit = lax.shift_right_logical(q_row, 4) & 3
    q_par = lax.shift_right_logical(q_row, 6)
    q_base = (q_row & 15) * 16 + q_par
    pick_early = (q_base + 2 * (q_unit + 2) == q_col).astype(BF16)
    pick_late = (q_base + 2 * jnp.where(q_unit < 2, q_unit, q_unit + 4) == q_col).astype(BF16)

    for p in range(TILES):
        count = jnp.int32(0)
        place = [jnp.int32(0)] * MOST
        valid = [jnp.int32(0)] * MOST
        for u in range(UNITS):
            hit = table[gy, u, 0] == p
            for m in range(MOST):
                take = hit & (count == m)
                place[m] = jnp.where(take, UNIT_ORDER.index(u), place[m])
                valid[m] = jnp.where(take, 1, valid[m])
            count = count + hit.astype(jnp.int32)
        for m in range(MOST):
            picks[p, m] = place[m]
            picks[p, MOST + m] = valid[m]

    pfull[...] = jnp.zeros((NX, RP), F32)
    pfull[:, 0:R] = start_ref[...]
    eye = (iota(square, 0) == iota(square, 1)).astype(BF16)
    hi, lo = split(pfull[...])
    start_t[0:RP, :] = mm_nt(eye, hi).astype(BF16)
    start_t[RP:, :] = mm_nt(eye, lo).astype(BF16)

    def y_copy(stage, side, c):
        at = pl.ds(c * CH, CH)
        out, into = (ylo_out, yhi_in) if side == 0 else (yhi_out, ylo_in)
        peer = row(wrap(gy + (ROWS - 1 if side == 0 else 1), ROWS))
        return pltpu.make_async_remote_copy(
            src_ref=out.at[stage, at], dst_ref=into.at[stage, at],
            send_sem=y_send.at[stage, side, c], recv_sem=y_recv.at[stage, side, c],
            device_id=peer, device_id_type=MESH,
        )

    def x_copy(stage, side):
        out, into = (xlo_out, xhi_in) if side == 0 else (xhi_out, xlo_in)
        peer = tile(wrap(me + (TILES - 1 if side == 0 else 1), TILES))
        return pltpu.make_async_remote_copy(
            src_ref=out.at[stage], dst_ref=into.at[stage],
            send_sem=x_send.at[stage, side], recv_sem=x_recv.at[stage, side],
            device_id=peer, device_id_type=MESH,
        )

    def pack_faces(stage, x, rows):
        faces = mm(face, rows.astype(BF16)).astype(BF16)
        for i in range(2):
            part = faces[:, i * 128 : (i + 1) * 128]
            ylo_out[stage, x + i] = part[0:32]
            yhi_out[stage, x + i] = part[32:64]

    def pair(ref, x):
        return jnp.concatenate([ref[:, x].reshape(128, 128), ref[:, x + 1].reshape(128, 128)], axis=1)

    def send_x(stage, e):
        xlo_out[stage] = e[:, 4:8].astype(BF16)
        xhi_out[stage] = e[:, TX : TX + 4].astype(BF16)
        for side in range(2):
            x_copy(stage, side).start()

    def receive_x(stage, e):
        for side in range(2):
            x_copy(stage, side).wait_recv()
        e[:, 0:4] = xlo_in[stage].astype(F32)
        e[:, TX + 4 : TX + 8] = xhi_in[stage].astype(F32)

    def along_xz(e, out, at, k, x):
        here = e[k, pl.ds(x + 4, 8)]
        hi, lo = split(here.reshape(128, 128))
        res = mm(jnp.concatenate([hi, lo], axis=1), cz[k])
        total = here + (res[:, 0:128] + res[:, 128:]).reshape(8, TY, NZ)
        v, s1 = viscosity[k], speeds[0, k]
        for m in range(1, 5):
            b, a = time_step * curve_weights[m - 1] * v, time_step * slope_weights[m - 1] * s1
            total = total + (b - a) * e[k, pl.ds(x + 4 + m, 8)] + (b + a) * e[k, pl.ds(x + 4 - m, 8)]
        out[k, pl.ds(x + at, 8)] = total

    def along_y(e, out, at):
        @pl.loop(0, TX // 2)
        def _(i):
            x = i * 2
            hi, lo = split(pair(e, x + 4))
            res = mm(wy[...], jnp.concatenate([hi, lo], axis=0))
            res = res[0:128] + res[128:]
            for n in range(2):
                out[:, x + at + n] = out[:, x + at + n] + res[:, n * 128 : (n + 1) * 128].reshape(V, TY, NZ)

    def from_halo(stage, x):
        rhs = jnp.concatenate(
            [jnp.concatenate([ylo_in[stage, x + n], yhi_in[stage, x + n]], axis=0) for n in range(2)], axis=1
        )
        res = mm(wh[...], rhs)
        return res[0:128] + res[128:]

    def bulk(stage, e, out, at):
        @pl.loop(0, V)
        def _(k):
            @pl.loop(1, TX // 8 - 1)
            def _(c):
                along_xz(e, out, at, k, c * 8)

        along_y_first = stage == 0
        if along_y_first:
            pass
        receive_x(stage, e)

        @pl.loop(0, V)
        def _(k):
            along_xz(e, out, at, k, 0)
            along_xz(e, out, at, k, TX - 8)

        along_y(e, out, at)

    load.wait()
    pl.semaphore_wait(barrier, TILES - 1 + ROWS - 1)
    send_x(0, e1)
    for c in CHUNK_ORDER:
        @pl.loop(0, CH // 2)
        def _(i):
            x = c * CH + i * 2
            pack_faces(0, x, pair(e1, x + 4))

        for side in range(2):
            y_copy(0, side, c).start()

    bulk(0, e1, e2, 4)
    for n, c in enumerate(CHUNK_ORDER):
        for side in range(2):
            y_copy(0, side, c).wait_recv()

        @pl.loop(0, CH // 2)
        def _(i):
            x = c * CH + i * 2
            rows = pair(e2, x + 4) + from_halo(0, x)
            for j in range(2):
                e2[:, x + 4 + j] = rows[:, j * 128 : (j + 1) * 128].reshape(V, TY, NZ)
            pack_faces(1, x, rows)

        for side in range(2):
            y_copy(1, side, c).start()
        if n == 1:
            send_x(1, e2)

    bulk(1, e2, acc, 0)

    def order_lines(pick, part):
        @pl.loop(0, V)
        def _(k):
            for g in range(TX // 16):
                at = pl.ds(g * 16, 16)
                lines = acc[k, at]
                if part == 0:
                    lines = 0.5 * (e1[k, pl.ds(g * 16 + 4, 16)] + lines)
                    acc[k, at] = lines
                got = mm(pick, lines.reshape(256, NZ).astype(BF16)).astype(BF16)
                for j in range(2):
                    for u in range(4):
                        r = (j * 4 + u) * 16
                        lane = part * 512 + u * 128
                        sbuf[k, j, g * 16 : g * 16 + 16, lane : lane + 128] = got[r : r + 16]

    def s_copy(part, d):
        peer = wrap(me + d, TILES)
        lanes = pl.ds(part * 512, 512)
        return pltpu.make_async_remote_copy(
            src_ref=sbuf.at[lax.div(peer, 2), lax.rem(peer, 2), :, lanes],
            dst_ref=srec.at[pl.ds(pl.multiple_of(me * TX, TX), TX), lanes],
            send_sem=s_send.at[part, d], recv_sem=s_recv.at[part, d],
            device_id=tile(peer), device_id_type=MESH,
        )

    def s_arrival(part, d):
        source = wrap(me + TILES - d, TILES)
        lanes = pl.ds(part * 512, 512)
        return pltpu.make_async_remote_copy(
            src_ref=sbuf.at[0, 0, :, lanes],
            dst_ref=srec.at[pl.ds(pl.multiple_of(source * TX, TX), TX), lanes],
            send_sem=s_send.at[part, d], recv_sem=s_recv.at[part, d],
            device_id=tile(source), device_id_type=MESH,
        )

    def s_local(part):
        lanes = pl.ds(part * 512, 512)
        return pltpu.make_async_copy(
            sbuf.at[lax.div(me, 2), lax.rem(me, 2), :, lanes],
            srec.at[pl.ds(pl.multiple_of(me * TX, TX), TX), lanes],
            s_own.at[part],
        )

    def send_lines(part):
        @pl.loop(1, TILES)
        def _(d):
            s_copy(part, d).start()

        s_local(part).start()

    def receive_lines(part):
        @pl.loop(1, TILES)
        def _(d):
            s_arrival(part, d).wait_recv()

        s_local(part).wait()

    def add_product(part):
        lanes = slice(part * 512, part * 512 + 512)
        res = mm(start_t[...], srec[:, lanes])
        hi, lo = split(res[0:RP] + res[RP:])
        right = jnp.concatenate([hi, lo], axis=0)

        @pl.loop(0, NX // 128)
        def _(i):
            at = pl.ds(pl.multiple_of(i * 128, 128), 128)
            got = mm_nt(srec[at, lanes], right)
            got = got[:, 0:RP] + got[:, RP:]
            if part == 0:
                pacc[at, :] = got
            else:
                got = pacc[at, :] + got
                pacc[at, :] = got
                psend[at, :] = got.astype(BF16)

    order_lines(pick_early, 0)
    send_lines(0)
    for c in CHUNK_ORDER:
        for side in range(2):
            y_copy(1, side, c).wait_recv()

        @pl.loop(0, CH // 2)
        def _(i):
            x = c * CH + i * 2
            rows = 0.5 * from_halo(1, x)
            for j in range(2):
                acc[:, x + j] = acc[:, x + j] + rows[:, j * 128 : (j + 1) * 128].reshape(V, TY, NZ)

    order_lines(pick_late, 1)
    send_lines(1)
    store = pltpu.make_async_copy(acc, final_hbm, final_sem)
    store.start()

    receive_lines(0)
    add_product(0)
    receive_lines(1)
    add_product(1)

    def p_copy(d, peer, source):
        return pltpu.make_async_remote_copy(
            src_ref=psend.at[pl.ds(pl.multiple_of(peer * TX, TX), TX)], dst_ref=prec.at[source],
            send_sem=p_send.at[d], recv_sem=p_recv.at[d], device_id=tile(peer), device_id_type=MESH,
        )

    mine = pl.ds(pl.multiple_of(me * TX, TX), TX)

    @pl.loop(1, TILES)
    def _(d):
        p_copy(d, wrap(me + d, TILES), me).start()

    prec[me] = psend[mine, :]

    @pl.loop(1, TILES)
    def _(d):
        p_copy(d, me, wrap(me + TILES - d, TILES)).wait_recv()

    total = prec[0].astype(F32)
    for i in range(1, TILES):
        total = total + prec[i].astype(F32)
    qrec[gy] = total

    def q_copy(d, peer, source):
        return pltpu.make_async_remote_copy(
            src_ref=qrec.at[gy], dst_ref=qrec.at[source],
            send_sem=q_send.at[d], recv_sem=q_recv.at[d], device_id=row(peer), device_id_type=MESH,
        )

    @pl.loop(1, ROWS)
    def _(d):
        q_copy(d, wrap(gy + d, ROWS), gy).start()

    @pl.loop(1, ROWS)
    def _(d):
        q_copy(d, gy, wrap(gy + ROWS - d, ROWS)).wait_recv()

    total = qrec[0]
    for i in range(1, ROWS):
        total = total + qrec[i]
    pfull[mine, :] = total

    def f_copy(d, peer, source):
        return pltpu.make_async_remote_copy(
            src_ref=pfull.at[mine], dst_ref=pfull.at[pl.ds(pl.multiple_of(source * TX, TX), TX)],
            send_sem=f_send.at[d], recv_sem=f_recv.at[d], device_id=tile(peer), device_id_type=MESH,
        )

    @pl.loop(1, TILES)
    def _(d):
        f_copy(d, wrap(me + d, TILES), me).start()

    @pl.loop(1, TILES)
    def _(d):
        f_copy(d, me, wrap(me + TILES - d, TILES)).wait_recv()

    product = pfull[...]
    turned = product.T
    prod_t[...] = turned
    norm = jnp.sum(jnp.sum(product * product, axis=0, keepdims=True), axis=1, keepdims=True)
    hi, lo = split(turned)
    inner = mm_nt(hi, hi) + (mm_nt(hi, lo) + mm_nt(lo, hi))
    inner = inner / norm
    ident = (iota(square, 0) == iota(square, 1)).astype(F32)
    chain = None
    for n in range(NEWTON):
        factor = 1.5 * ident - 0.5 * inner
        chain = factor if n == 0 else both(factor, chain)
        if n < NEWTON - 1:
            inner = both(factor, both(inner, factor))
    basis_t = both(chain, prod_t[...]) / jnp.sqrt(norm)
    half = basis_t.astype(BF16)
    for u in range(UNITS):
        got = mm(half, srec[:, u * 128 : (u + 1) * 128])
        blocks[u] = got[0:R].astype(BF16)

    @pl.loop(0, TILES)
    def _(p):
        for m in range(MOST):
            got = blocks[picks[p, m]]
            csend[p, m] = jnp.where(picks[p, MOST + m] == 1, got, jnp.zeros_like(got))

    def c_copy(d, peer, source):
        return pltpu.make_async_remote_copy(
            src_ref=csend.at[peer], dst_ref=crec.at[source],
            send_sem=c_send.at[d], recv_sem=c_recv.at[d], device_id=tile(peer), device_id_type=MESH,
        )

    @pl.loop(1, TILES)
    def _(d):
        c_copy(d, wrap(me + d, TILES), me).start()

    crec[me] = csend[me]

    @pl.loop(1, TILES)
    def _(d):
        c_copy(d, me, wrap(me + TILES - d, TILES)).wait_recv()

    out = pltpu.make_async_copy(crec, core_hbm, core_sem)
    out.start()

    for stage in range(2):
        for side in range(2):
            x_copy(stage, side).wait_send()
            for c in range(CHUNKS):
                y_copy(stage, side, c).wait_send()

    @pl.loop(1, TILES)
    def _(d):
        peer = wrap(me + d, TILES)
        for part in range(2):
            s_copy(part, d).wait_send()
        p_copy(d, peer, me).wait_send()
        f_copy(d, peer, me).wait_send()
        c_copy(d, peer, me).wait_send()

    @pl.loop(1, ROWS)
    def _(d):
        q_copy(d, wrap(gy + d, ROWS), gy).wait_send()

    store.wait()
    out.wait()


def unpack(core_ref, out_ref):
    for m in range(MOST):
        for s in range(TILES):
            out_ref[m, :, s, :] = core_ref[s, m].astype(F32)


def on_device(flow_state, speeds, viscosity, reaction, start_basis, slab_table):
    dma = pltpu.SemaphoreType.DMA
    vmem = pltpu.VMEM
    halo_y = vmem((2, TX, 32, NZ), BF16)
    halo_x = vmem((2, V, 4, TY, NZ), BF16)
    hbm = pl.BlockSpec(memory_space=pl.ANY)
    smem = pl.BlockSpec(memory_space=pltpu.SMEM)
    final_state, cores = pl.pallas_call(
        kernel,
        name="sections_and_core",
        out_shape=(
            jax.ShapeDtypeStruct((V, TX, TY, NZ), F32),
            jax.ShapeDtypeStruct((TILES, MOST, R, NZ), BF16),
        ),
        in_specs=[hbm, smem, smem, smem, pl.BlockSpec(memory_space=pltpu.VMEM), smem],
        out_specs=(hbm, hbm),
        scratch_shapes=[
            vmem((V, TX + 8, TY, NZ), F32),
            vmem((V, TX + 8, TY, NZ), F32),
            vmem((V, TX, TY, NZ), F32),
            halo_y, halo_y, halo_y, halo_y,
            halo_x, halo_x, halo_x, halo_x,
            vmem((V, 2, TX, UNITS * NZ), BF16),
            vmem((NX, UNITS * NZ), BF16),
            vmem((V, 256, 256), BF16),
            vmem((256, 256), BF16),
            vmem((256, 64), BF16),
            vmem((2 * RP, NX), BF16),
            vmem((NX, RP), F32),
            vmem((NX, RP), BF16),
            vmem((TILES, TX, RP), BF16),
            vmem((ROWS, TX, RP), F32),
            vmem((NX, RP), F32),
            vmem((RP, NX), F32),
            vmem((UNITS, R, NZ), BF16),
            vmem((TILES, MOST, R, NZ), BF16),
            vmem((TILES, MOST, R, NZ), BF16),
            pltpu.SMEM((TILES, 2 * MOST), jnp.int32),
            dma(()), dma(()), dma(()),
            dma((2, 2, CHUNKS)), dma((2, 2, CHUNKS)), dma((2, 2)), dma((2, 2)),
            dma((2, TILES)), dma((2, TILES)), dma((2,)),
            dma((TILES,)), dma((TILES,)), dma((ROWS,)), dma((ROWS,)),
            dma((TILES,)), dma((TILES,)), dma((TILES,)), dma((TILES,)),
        ],
        compiler_params=pltpu.CompilerParams(
            collective_id=0, has_side_effects=True, vmem_limit_bytes=56 * 1024 * 1024
        ),
    )(flow_state, speeds, viscosity, reaction, start_basis, slab_table)
    core_slots = pl.pallas_call(
        unpack,
        name="unpack_core",
        out_shape=jax.ShapeDtypeStruct((MOST, R, TILES, NZ), F32),
        in_specs=[pl.BlockSpec(memory_space=pltpu.VMEM)],
        out_specs=pl.BlockSpec(memory_space=pltpu.VMEM),
        compiler_params=pltpu.CompilerParams(vmem_limit_bytes=32 * 1024 * 1024),
    )(cores)
    return final_state, core_slots.reshape(MOST, R, V, 2, NZ)


def solution(mesh):
    field = P(None, ("grp", "gx"), "gy", None)
    return jax.shard_map(
        on_device,
        mesh=mesh,
        in_specs=(field, P(), P(), P(), P(), P()),
        out_specs=(field, P(("grp", "gx", "gy"), None, None, None, None)),
        check_vma=False,
    )
```

```python
import jax
import jax.numpy as jnp
from jax import lax
from jax.experimental import pallas as pl
from jax.experimental.pallas import tpu as pltpu
from jax.sharding import PartitionSpec as P

V = 8
NX = 768
R = 96
RP = 128
NZ = 128
TX = 48
TY = 16
TILES = 16
ROWS = 8
UNITS = 8
MOST = 2
NEWTON = 5
CH = 16
CHUNKS = TX // CH
CHUNK_ORDER = (1, 0, 2)
PEERS = (
    (2, 1, 0), (1, 0, 0), (3, 0, 0), (0, 1, 0), (2, 1, 1), (1, 0, 1), (3, 0, 1), (0, 1, 1),
    (2, 0, 0), (1, 1, 0), (3, 1, 0), (2, 0, 1), (1, 1, 1), (3, 1, 1), (0, 0, 1),
)
SAME_CORE = tuple(n for n in range(15) if PEERS[n][2] == 0)
PARTNER = 14
EARLY = (2, 3, 4, 5)
LATE = (0, 1, 6, 7)
UNIT_ORDER = EARLY + LATE

slope_weights = (0.8, -0.2, 4.0 / 105.0, -1.0 / 280.0)
curve_weights = (1.6, -0.2, 8.0 / 315.0, -1.0 / 560.0)
curve_center = -205.0 / 72.0
time_step = 0.2

MESH = pl.DeviceIdType.MESH
F32 = jnp.float32
BF16 = jnp.bfloat16
NT = (((1,), (1,)), ((), ()))


def split(x):
    high = x.astype(BF16)
    return high, (x - high.astype(F32)).astype(BF16)


def mm(a, b):
    return jnp.dot(a, b, preferred_element_type=F32)


def mm_nt(a, b):
    return lax.dot_general(a, b, NT, preferred_element_type=F32)


def both(a, b):

    ah, al = split(a)
    bh, bl = split(b)
    left = jnp.concatenate([ah, ah, al], axis=1)
    right = jnp.concatenate([bh, bl, bh], axis=0)
    return mm(left, right)


def iota(shape, dim):
    return lax.broadcasted_iota(jnp.int32, shape, dim)


def curve_of(distance):
    out = jnp.zeros(distance.shape, F32)
    for m in range(1, 5):
        hit = (distance == m) | (distance == -m)
        out = jnp.where(hit, time_step * curve_weights[m - 1], out)
    return out


def slope_of(distance):
    out = jnp.zeros(distance.shape, F32)
    for m in range(1, 5):
        out = jnp.where(distance == m, -time_step * slope_weights[m - 1], out)
        out = jnp.where(distance == -m, time_step * slope_weights[m - 1], out)
    return out


def kernel(
    flow_hbm, speeds, viscosity, reaction, start_ref, table,
    acc, crec,
    e1, e2,
    ylo_out, yhi_out, ylo_in, yhi_in,
    xlo_out, xhi_out, xlo_in, xhi_in,
    sbuf, srec,
    cz, wy, wh,
    start_t, pacc, psend, prec, qrec, pfull, prod_t, blocks, csend,
    picks,
    load_sem,
    y_send, y_recv, x_send, x_recv, s_send, s_recv,
    p_send, p_recv, q_send, q_recv, f_send, f_recv, g_send, g_recv, c_send, c_recv,
):
    grp, gx, gy = (lax.axis_index(a) for a in ("grp", "gx", "gy"))
    me = grp * 4 + gx

    def tile(i):
        return (lax.div(i, 4), lax.rem(i, 4), gy)

    def tile_at(n, back=False):
        dg, dz, dc = PEERS[n]
        g = lax.rem(grp + (4 - dg if back else dg), 4)
        x = lax.rem(lax.div(gx, 2) + dz, 2) * 2 + lax.rem(gx + dc, 2)
        return g, x, g * 4 + x

    def row(i):
        return (grp, gx, i)

    def wrap(i, n):
        return lax.rem(i, n)

    barrier = pltpu.get_barrier_semaphore()

    @pl.loop(1, TILES)
    def _(d):
        pl.semaphore_signal(barrier, inc=1, device_id=tile(wrap(me + d, TILES)), device_id_type=MESH)

    @pl.loop(1, ROWS)
    def _(d):
        pl.semaphore_signal(barrier, inc=1, device_id=row(wrap(gy + d, ROWS)), device_id_type=MESH)

    load = pltpu.make_async_copy(flow_hbm, e1.at[:, 4 : 4 + TX], load_sem)
    load.start()

    f_row, f_col = iota((64, 128), 0), iota((64, 128), 1)
    f_src = (lax.shift_right_logical(f_row, 2) & 7) * 16 + (f_row & 3) + lax.shift_right_logical(f_row, 5) * 12
    face = (f_src == f_col).astype(BF16)

    q_row, q_col = iota((128, 256), 0), iota((128, 256), 1)
    q_unit = lax.shift_right_logical(q_row, 4) & 3
    q_par = lax.shift_right_logical(q_row, 6)
    q_base = (q_row & 15) * 16 + q_par
    pick_early = (q_base + 2 * (q_unit + 2) == q_col).astype(BF16)
    pick_late = (q_base + 2 * jnp.where(q_unit < 2, q_unit, q_unit + 4) == q_col).astype(BF16)

    def y_copy(stage, side):
        out, into = (ylo_out, yhi_in) if side == 0 else (yhi_out, ylo_in)
        peer = row(wrap(gy + (ROWS - 1 if side == 0 else 1), ROWS))
        return pltpu.make_async_remote_copy(
            src_ref=out.at[stage], dst_ref=into.at[stage],
            send_sem=y_send.at[stage, side], recv_sem=y_recv.at[stage, side],
            device_id=peer, device_id_type=MESH,
        )

    def x_copy(stage, side):
        out, into = (xlo_out, xhi_in) if side == 0 else (xhi_out, xlo_in)
        peer = tile(wrap(me + (TILES - 1 if side == 0 else 1), TILES))
        return pltpu.make_async_remote_copy(
            src_ref=out.at[stage], dst_ref=into.at[stage],
            send_sem=x_send.at[stage, side], recv_sem=x_recv.at[stage, side],
            device_id=peer, device_id_type=MESH,
        )

    def wide(ref, x, n):
        return jnp.concatenate([ref[:, x + i].reshape(128, 128) for i in range(n)], axis=1)

    def pack_faces(stage, x, rows, n):
        faces = mm(face, rows.astype(BF16)).astype(BF16)
        for i in range(n):
            part = faces[:, i * 128 : (i + 1) * 128]
            ylo_out[stage, x + i] = part[0:32]
            yhi_out[stage, x + i] = part[32:64]

    def make_x(stage, e):
        xlo_out[stage] = e[:, 4:8].astype(BF16)
        xhi_out[stage] = e[:, TX : TX + 4].astype(BF16)

    def send_x(stage):
        for side in range(2):
            x_copy(stage, side).start()

    def receive_x(stage, e):
        for side in range(2):
            x_copy(stage, side).wait_recv()
        e[:, 0:4] = xlo_in[stage].astype(F32)
        e[:, TX + 4 : TX + 8] = xhi_in[stage].astype(F32)

    def along_xz(e, out, at, k, x, n):
        here = e[k, pl.ds(x + 4, n)]
        hi, lo = split(here.reshape(n * TY, NZ))
        res = mm(jnp.concatenate([hi, lo], axis=1), cz[k])
        total = here + (res[:, 0:128] + res[:, 128:]).reshape(n, TY, NZ)
        v, s1 = viscosity[k], speeds[0, k]
        for m in range(1, 5):
            b, a = time_step * curve_weights[m - 1] * v, time_step * slope_weights[m - 1] * s1
            total = total + (b - a) * e[k, pl.ds(x + 4 + m, n)] + (b + a) * e[k, pl.ds(x + 4 - m, n)]
        out[k, pl.ds(x + at, n)] = total

    def along_y(e, out, at, x):
        hi, lo = split(wide(e, x + 4, 8))
        res = mm(wy[...], jnp.concatenate([hi, lo], axis=0))
        res = res[0:128] + res[128:]
        for n in range(8):
            out[:, x + at + n] = out[:, x + at + n] + res[:, n * 128 : (n + 1) * 128].reshape(V, TY, NZ)

    def from_halo(stage, x, n):
        rhs = jnp.concatenate(
            [jnp.concatenate([ylo_in[stage, x + i], yhi_in[stage, x + i]], axis=0) for i in range(n)], axis=1
        )
        res = mm(wh[...], rhs)
        return res[0:128] + res[128:]

    load.wait()
    make_x(0, e1)

    @pl.loop(0, TX // 8)
    def _(i):
        pack_faces(0, i * 8, wide(e1, i * 8 + 4, 8), 8)

    square = (128, 128)
    turn = (iota(square, 0) - iota(square, 1)) & 127
    turn = jnp.where(turn > 64, turn - 128, turn)
    z_curve, z_slope = curve_of(turn), slope_of(turn)
    y_shape = (TY, 128)
    y_dist = (iota(y_shape, 1) & 15) - iota(y_shape, 0)
    y_var = lax.shift_right_logical(iota(y_shape, 1), 4)
    y_curve = jnp.where(y_dist == 0, time_step * 3.0 * curve_center, curve_of(y_dist))
    y_slope = slope_of(y_dist)
    h_shape = (TY, 64)
    h_col = iota(h_shape, 1)
    h_dist = (h_col & 3) - 4 + lax.shift_right_logical(h_col, 5) * 20 - iota(h_shape, 0)
    h_var = lax.shift_right_logical(h_col, 2) & 7
    h_curve, h_slope = curve_of(h_dist), slope_of(h_dist)

    @pl.loop(0, V)
    def _(k):
        v, s2, s3 = viscosity[k], speeds[1, k], speeds[2, k]
        ch, cl = split(v * z_curve + s3 * z_slope)
        cz[k] = jnp.concatenate(
            [jnp.concatenate([ch, cl], axis=1), jnp.concatenate([ch, jnp.zeros_like(cl)], axis=1)], axis=0
        )
        w = jnp.where(y_var == k, v * y_curve + s2 * y_slope, 0.0)
        for j in range(V):
            w = w + jnp.where((y_var == j) & (y_dist == 0), time_step * reaction[k, j], 0.0)
        hi, lo = split(w)
        at = pl.ds(pl.multiple_of(k * TY, TY), TY)
        at2 = pl.ds(pl.multiple_of(128 + k * TY, TY), TY)
        wy[at, :] = jnp.concatenate([hi, hi], axis=1)
        wy[at2, :] = jnp.concatenate([lo, jnp.zeros_like(lo)], axis=1)
        hi, lo = split(jnp.where(h_var == k, v * h_curve + s2 * h_slope, 0.0))
        wh[at, :] = hi
        wh[at2, :] = lo

    pl.semaphore_wait(barrier, TILES - 1 + ROWS - 1)
    send_x(0)
    for side in range(2):
        y_copy(0, side).start()

    for p in range(TILES):
        count = jnp.int32(0)
        place = [jnp.int32(0)] * MOST
        valid = [jnp.int32(0)] * MOST
        for u in range(UNITS):
            hit = table[gy, 0, u] == p
            for m in range(MOST):
                take = hit & (count == m)
                place[m] = jnp.where(take, UNIT_ORDER.index(u), place[m])
                valid[m] = jnp.where(take, 1, valid[m])
            count = count + hit.astype(jnp.int32)
        for m in range(MOST):
            picks[p, m] = place[m]
            picks[p, MOST + m] = valid[m]

    hi, lo = split(start_ref[...])
    start_t[...] = jnp.zeros((2 * RP, NX), BF16)
    start_t[0:R, :] = hi
    start_t[RP : RP + R, :] = lo

    @pl.loop(0, V, unroll=2)
    def _(k):
        along_xz(e1, e2, 4, k, 8, 16)
        along_xz(e1, e2, 4, k, 24, 16)

    @pl.loop(1, TX // 8 - 1)
    def _(i):
        along_y(e1, e2, 4, i * 8)

    receive_x(0, e1)

    @pl.loop(0, V, unroll=2)
    def _(k):
        along_xz(e1, e2, 4, k, 0, 8)
        along_xz(e1, e2, 4, k, TX - 8, 8)

    for x in (0, TX - 8):
        along_y(e1, e2, 4, x)

    for side in range(2):
        y_copy(0, side).wait_recv()

    @pl.loop(0, TX // 8)
    def _(i):
        x = i * 8
        rows = wide(e2, x + 4, 8) + from_halo(0, x, 8)
        for j in range(8):
            e2[:, x + 4 + j] = rows[:, j * 128 : (j + 1) * 128].reshape(V, TY, NZ)
        pack_faces(1, x, rows, 8)

    make_x(1, e2)
    send_x(1)
    for side in range(2):
        y_copy(1, side).start()

    def order_lines(part, c):
        pick = pick_early if part == 0 else pick_late
        at = slice(c * CH, c * CH + CH)

        @pl.loop(0, V // 2, unroll=2)
        def _(i):
            both_k = []
            for k in (i * 2, i * 2 + 1):
                lines = acc[k, at]
                if part == 0:
                    lines = 0.5 * (e1[k, c * CH + 4 : c * CH + CH + 4] + lines)
                    acc[k, at] = lines
                both_k.append(lines.reshape(CH * TY, NZ).astype(BF16))
            got = mm(pick, jnp.concatenate(both_k, axis=1)).astype(BF16)
            for n in range(2):
                for j in range(2):
                    for u in range(4):
                        r = (j * 4 + u) * 16
                        lane = part * 512 + u * 128
                        sbuf[i * 2 + n, j, at, lane : lane + 128] = got[r : r + 16, n * 128 : n * 128 + 128]

    def s_copy(part, n, arrival):
        g, x, peer = tile_at(n, back=arrival)
        source = peer if arrival else me
        lanes = pl.ds(part * 512, 512)
        return pltpu.make_async_remote_copy(
            src_ref=sbuf.at[lax.div(peer, 2), lax.rem(peer, 2), :, lanes],
            dst_ref=srec.at[pl.ds(pl.multiple_of(source * TX, TX), TX), lanes],
            send_sem=s_send.at[part, n], recv_sem=s_recv.at[part, n],
            device_id=(g, x, gy), device_id_type=MESH,
        )

    mine = pl.ds(pl.multiple_of(me * TX, TX), TX)

    def send_lines(part):
        for n in range(15):
            s_copy(part, n, False).start()
        lanes = slice(part * 512, part * 512 + 512)
        srec[mine, lanes] = sbuf[lax.div(me, 2), lax.rem(me, 2), :, lanes]

    def receive_lines(part):
        for n in range(15):
            s_copy(part, n, True).wait_recv()

    def add_product(part):
        lanes = slice(part * 512, part * 512 + 512)
        res = mm(start_t[...], srec[:, lanes])
        hi, lo = split(res[0:RP] + res[RP:])
        right = jnp.concatenate([hi, lo], axis=0)

        @pl.loop(0, NX // 256)
        def _(i):
            at = pl.ds(pl.multiple_of(i * 256, 256), 256)
            got = mm_nt(srec[at, lanes], right)
            got = got[:, 0:RP] + got[:, RP:]
            if part == 0:
                pacc[at, :] = got
            else:
                got = pacc[at, :] + got
                pacc[at, :] = got
                psend[at, :] = got.astype(BF16)

    for n, c in enumerate(CHUNK_ORDER):
        if n == 1:
            receive_x(1, e2)

        @pl.loop(0, V, unroll=4)
        def _(k):
            along_xz(e2, acc, 0, k, c * CH, CH)

        for i in range(CH // 8):
            along_y(e2, acc, 0, c * CH + i * 8)
        order_lines(0, c)

    for side in range(2):
        y_copy(1, side).wait_recv()
    send_lines(0)
    for c in range(CHUNKS):
        for i in range(CH // 8):
            x = c * CH + i * 8
            rows = 0.5 * from_halo(1, x, 8)
            for j in range(8):
                acc[:, x + j] = acc[:, x + j] + rows[:, j * 128 : (j + 1) * 128].reshape(V, TY, NZ)
        order_lines(1, c)

    send_lines(1)
    receive_lines(0)
    add_product(0)
    receive_lines(1)
    add_product(1)

    def p_copy(n, arrival):
        g, x, peer = tile_at(n, back=arrival)
        to, source = (me, peer) if arrival else (peer, me)
        return pltpu.make_async_remote_copy(
            src_ref=psend.at[pl.ds(pl.multiple_of(to * TX, TX), TX)], dst_ref=prec.at[source],
            send_sem=p_send.at[n], recv_sem=p_recv.at[n], device_id=(g, x, gy), device_id_type=MESH,
        )

    for n in range(15):
        p_copy(n, False).start()
    prec[me] = psend[mine, :]
    for n in range(15):
        p_copy(n, True).wait_recv()

    total = prec[0].astype(F32)
    for i in range(1, TILES):
        total = total + prec[i].astype(F32)
    qrec[gy] = total

    def q_copy(d, peer, source):
        return pltpu.make_async_remote_copy(
            src_ref=qrec.at[gy], dst_ref=qrec.at[source],
            send_sem=q_send.at[d], recv_sem=q_recv.at[d], device_id=row(peer), device_id_type=MESH,
        )

    @pl.loop(1, ROWS)
    def _(d):
        q_copy(d, wrap(gy + d, ROWS), gy).start()

    @pl.loop(1, ROWS)
    def _(d):
        q_copy(d, gy, wrap(gy + ROWS - d, ROWS)).wait_recv()

    total = qrec[0]
    for i in range(1, ROWS):
        total = total + qrec[i]
    pfull[mine, :] = total

    def rows_of(i):
        return pl.ds(pl.multiple_of(i * TX, TX), TX)

    def f_copy(n, arrival):
        g, x, peer = tile_at(n, back=arrival)
        at = rows_of(peer if arrival else me)
        return pltpu.make_async_remote_copy(
            src_ref=pfull.at[at], dst_ref=pfull.at[at],
            send_sem=f_send.at[n], recv_sem=f_recv.at[n], device_id=(g, x, gy), device_id_type=MESH,
        )

    def f_pass(n, arrival):
        g, x, peer = tile_at(n, back=True)
        _, x2, partner = tile_at(PARTNER)
        at = rows_of(peer - lax.rem(gx, 2) + lax.rem(x2, 2) if arrival else peer)
        return pltpu.make_async_remote_copy(
            src_ref=pfull.at[at], dst_ref=pfull.at[at],
            send_sem=g_send.at[n], recv_sem=g_recv.at[n], device_id=(grp, x2, gy), device_id_type=MESH,
        )

    for n in SAME_CORE + (PARTNER,):
        f_copy(n, False).start()
    for n in SAME_CORE:
        f_copy(n, True).wait_recv()
        f_pass(n, False).start()
    f_copy(PARTNER, True).wait_recv()
    for n in SAME_CORE:
        f_pass(n, True).wait_recv()

    product = pfull[...]
    turned = product.T
    prod_t[...] = turned
    norm = jnp.sum(jnp.sum(product * product, axis=0, keepdims=True), axis=1, keepdims=True)
    hi, lo = split(turned)
    inner = mm_nt(hi, hi) + (mm_nt(hi, lo) + mm_nt(lo, hi))
    inner = inner / norm
    ident = (iota(square, 0) == iota(square, 1)).astype(F32)
    chain = None
    for n in range(NEWTON):
        factor = 1.5 * ident - 0.5 * inner
        chain = factor if n == 0 else both(factor, chain)
        if n < NEWTON - 1:
            inner = both(factor, both(inner, factor))
    basis_t = both(chain, prod_t[...]) / jnp.sqrt(norm)
    half = basis_t.astype(BF16)
    for u in range(UNITS):
        got = mm(half, srec[:, u * 128 : (u + 1) * 128])
        blocks[u] = got[0:R].astype(BF16)

    @pl.loop(0, TILES)
    def _(p):
        for m in range(MOST):
            got = blocks[picks[p, m]]
            csend[p, m] = jnp.where(picks[p, MOST + m] == 1, got, jnp.zeros_like(got))

    def c_copy(n, arrival):
        g, x, peer = tile_at(n, back=arrival)
        to, source = (me, peer) if arrival else (peer, me)
        return pltpu.make_async_remote_copy(
            src_ref=csend.at[to], dst_ref=crec.at[source],
            send_sem=c_send.at[n], recv_sem=c_recv.at[n], device_id=(g, x, gy), device_id_type=MESH,
        )

    for n in range(15):
        c_copy(n, False).start()
    crec[me] = csend[me]
    for n in range(15):
        c_copy(n, True).wait_recv()

    for stage in range(2):
        for side in range(2):
            x_copy(stage, side).wait_send()
            y_copy(stage, side).wait_send()

    for n in range(15):
        for part in range(2):
            s_copy(part, n, False).wait_send()
        p_copy(n, False).wait_send()
        c_copy(n, False).wait_send()
    for n in SAME_CORE:
        f_copy(n, False).wait_send()
        f_pass(n, False).wait_send()
    f_copy(PARTNER, False).wait_send()

    @pl.loop(1, ROWS)
    def _(d):
        q_copy(d, wrap(gy + d, ROWS), gy).wait_send()


def unpack(final_ref, core_ref, final_out, out_hbm, out, final_sem, store_sem):
    final = pltpu.make_async_copy(final_ref, final_out, final_sem)
    final.start()
    stores = [pltpu.make_async_copy(out.at[m], out_hbm.at[m], store_sem.at[m]) for m in range(MOST)]
    for m in range(MOST):
        for s in range(TILES):
            out[m, :, s, :] = core_ref[s, m].astype(F32)
        stores[m].start()
    final.wait()
    for store in stores:
        store.wait()


def on_device(flow_state, speeds, viscosity, reaction, start_basis, slab_table):
    dma = pltpu.SemaphoreType.DMA
    vmem = pltpu.VMEM
    halo_y = vmem((2, TX, 32, NZ), BF16)
    halo_x = vmem((2, V, 4, TY, NZ), BF16)
    hbm = pl.BlockSpec(memory_space=pl.ANY)
    smem = pl.BlockSpec(memory_space=pltpu.SMEM)
    vm = pl.BlockSpec(memory_space=pltpu.VMEM)
    final_state, cores = pl.pallas_call(
        kernel,
        name="sections_and_core",
        out_shape=(vmem((V, TX, TY, NZ), F32), vmem((TILES, MOST, R, NZ), BF16)),
        in_specs=[hbm, smem, smem, smem, vm, smem],
        out_specs=(vm, vm),
        scratch_shapes=[
            vmem((V, TX + 8, TY, NZ), F32),
            vmem((V, TX + 8, TY, NZ), F32),
            halo_y, halo_y, halo_y, halo_y,
            halo_x, halo_x, halo_x, halo_x,
            vmem((V, 2, TX, UNITS * NZ), BF16),
            vmem((NX, UNITS * NZ), BF16),
            vmem((V, 256, 256), BF16),
            vmem((256, 256), BF16),
            vmem((256, 64), BF16),
            vmem((2 * RP, NX), BF16),
            vmem((NX, RP), F32),
            vmem((NX, RP), BF16),
            vmem((TILES, TX, RP), BF16),
            vmem((ROWS, TX, RP), F32),
            vmem((NX, RP), F32),
            vmem((RP, NX), F32),
            vmem((UNITS, R, NZ), BF16),
            vmem((TILES, MOST, R, NZ), BF16),
            pltpu.SMEM((TILES, 2 * MOST), jnp.int32),
            dma(()),
            dma((2, 2)), dma((2, 2)), dma((2, 2)), dma((2, 2)),
            dma((2, 15)), dma((2, 15)),
            dma((15,)), dma((15,)), dma((ROWS,)), dma((ROWS,)),
            dma((15,)), dma((15,)), dma((15,)), dma((15,)), dma((15,)), dma((15,)),
        ],
        compiler_params=pltpu.CompilerParams(
            collective_id=0, has_side_effects=True, vmem_limit_bytes=60 * 1024 * 1024
        ),
    )(flow_state, speeds, viscosity, reaction, start_basis.T, slab_table.transpose(0, 2, 1))
    final_state, core_slots = pl.pallas_call(
        unpack,
        name="unpack_core",
        out_shape=(
            jax.ShapeDtypeStruct((V, TX, TY, NZ), F32),
            jax.ShapeDtypeStruct((MOST, R, TILES, NZ), F32),
        ),
        in_specs=[vm, vm],
        out_specs=(hbm, hbm),
        scratch_shapes=[
            vmem((MOST, R, TILES, NZ), F32),
            dma(()), dma((MOST,)),
        ],
        compiler_params=pltpu.CompilerParams(vmem_limit_bytes=32 * 1024 * 1024),
    )(final_state, cores)
    return final_state, core_slots.reshape(MOST, R, V, 2, NZ)


def solution(mesh):
    field = P(None, ("grp", "gx"), "gy", None)
    return jax.shard_map(
        on_device,
        mesh=mesh,
        in_specs=(field, P(), P(), P(), P(), P()),
        out_specs=(field, P(("grp", "gx", "gy"), None, None, None, None)),
        check_vma=False,
    )
```

```python
import jax
import jax.numpy as jnp
from jax import lax
from jax.experimental import pallas as pl
from jax.experimental.pallas import tpu as pltpu
from jax.sharding import PartitionSpec as P

V = 8
NX = 768
R = 96
RP = 128
NZ = 128
TX = 48
TY = 16
TILES = 16
ROWS = 8
UNITS = 8
MOST = 2
NEWTON = 5
CH = 16
CHUNKS = TX // CH
PEERS = (
    (2, 1, 0), (1, 0, 0), (3, 0, 0), (0, 1, 0), (2, 1, 1), (1, 0, 1), (3, 0, 1), (0, 1, 1),
    (2, 0, 0), (1, 1, 0), (3, 1, 0), (2, 0, 1), (1, 1, 1), (3, 1, 1), (0, 0, 1),
)
SAME_CORE = tuple(n for n in range(15) if PEERS[n][2] == 0)
PARTNER = 14
EARLY = (2, 3, 4, 5)
LATE = (0, 1, 6, 7)
UNIT_ORDER = EARLY + LATE

slope_weights = (0.8, -0.2, 4.0 / 105.0, -1.0 / 280.0)
curve_weights = (1.6, -0.2, 8.0 / 315.0, -1.0 / 560.0)
curve_center = -205.0 / 72.0
time_step = 0.2

MESH = pl.DeviceIdType.MESH
F32 = jnp.float32
BF16 = jnp.bfloat16
NT = (((1,), (1,)), ((), ()))


def split(x):
    high = x.astype(BF16)
    return high, (x - high.astype(F32)).astype(BF16)


def mm(a, b):
    return jnp.dot(a, b, preferred_element_type=F32)


def mm_nt(a, b):
    return lax.dot_general(a, b, NT, preferred_element_type=F32)


def both(a, b):

    ah, al = split(a)
    bh, bl = split(b)
    left = jnp.concatenate([ah, ah, al], axis=1)
    right = jnp.concatenate([bh, bl, bh], axis=0)
    return mm(left, right)


def iota(shape, dim):
    return lax.broadcasted_iota(jnp.int32, shape, dim)


def curve_of(distance):
    out = jnp.zeros(distance.shape, F32)
    for m in range(1, 5):
        hit = (distance == m) | (distance == -m)
        out = jnp.where(hit, time_step * curve_weights[m - 1], out)
    return out


def slope_of(distance):
    out = jnp.zeros(distance.shape, F32)
    for m in range(1, 5):
        out = jnp.where(distance == m, -time_step * slope_weights[m - 1], out)
        out = jnp.where(distance == -m, time_step * slope_weights[m - 1], out)
    return out


def kernel(
    flow_hbm, speeds, viscosity, reaction, start_ref, table,
    acc, crec,
    e1, e2,
    ylo_out, yhi_out, ylo_in, yhi_in,
    xlo_out, xhi_out, xlo_in, xhi_in,
    sbuf, srec,
    cz, wy, wh,
    start_t, pacc, psend, prec, qrec, pfull, prod_t, blocks, csend,
    picks,
    load_sem,
    y_send, y_recv, x_send, x_recv, s_send, s_recv,
    p_send, p_recv, q_send, q_recv, f_send, f_recv, g_send, g_recv, c_send, c_recv,
):
    grp, gx, gy = (lax.axis_index(a) for a in ("grp", "gx", "gy"))
    me = grp * 4 + gx

    def tile(i):
        return (lax.div(i, 4), lax.rem(i, 4), gy)

    def tile_at(n, back=False):
        dg, dz, dc = PEERS[n]
        g = lax.rem(grp + (4 - dg if back else dg), 4)
        x = lax.rem(lax.div(gx, 2) + dz, 2) * 2 + lax.rem(gx + dc, 2)
        return g, x, g * 4 + x

    def row(i):
        return (grp, gx, i)

    def wrap(i, n):
        return lax.rem(i, n)

    barrier = pltpu.get_barrier_semaphore()

    @pl.loop(1, TILES)
    def _(d):
        pl.semaphore_signal(barrier, inc=1, device_id=tile(wrap(me + d, TILES)), device_id_type=MESH)

    @pl.loop(1, ROWS)
    def _(d):
        pl.semaphore_signal(barrier, inc=1, device_id=row(wrap(gy + d, ROWS)), device_id_type=MESH)

    load = pltpu.make_async_copy(flow_hbm, e1.at[:, 4 : 4 + TX], load_sem)
    load.start()

    f_row, f_col = iota((64, 128), 0), iota((64, 128), 1)
    f_src = (lax.shift_right_logical(f_row, 2) & 7) * 16 + (f_row & 3) + lax.shift_right_logical(f_row, 5) * 12
    face = (f_src == f_col).astype(BF16)

    q_row, q_col = iota((128, 256), 0), iota((128, 256), 1)
    q_unit = lax.shift_right_logical(q_row, 4) & 3
    q_par = lax.shift_right_logical(q_row, 6)
    q_base = (q_row & 15) * 16 + q_par
    pick_early = (q_base + 2 * (q_unit + 2) == q_col).astype(BF16)
    pick_late = (q_base + 2 * jnp.where(q_unit < 2, q_unit, q_unit + 4) == q_col).astype(BF16)

    def y_copy(stage, side):
        out, into = (ylo_out, yhi_in) if side == 0 else (yhi_out, ylo_in)
        peer = row(wrap(gy + (ROWS - 1 if side == 0 else 1), ROWS))
        return pltpu.make_async_remote_copy(
            src_ref=out.at[stage], dst_ref=into.at[stage],
            send_sem=y_send.at[stage, side], recv_sem=y_recv.at[stage, side],
            device_id=peer, device_id_type=MESH,
        )

    def x_copy(stage, side):
        out, into = (xlo_out, xhi_in) if side == 0 else (xhi_out, xlo_in)
        peer = tile(wrap(me + (TILES - 1 if side == 0 else 1), TILES))
        return pltpu.make_async_remote_copy(
            src_ref=out.at[stage], dst_ref=into.at[stage],
            send_sem=x_send.at[stage, side], recv_sem=x_recv.at[stage, side],
            device_id=peer, device_id_type=MESH,
        )

    def wide(ref, x, n):
        return jnp.concatenate([ref[:, x + i].reshape(128, 128) for i in range(n)], axis=1)

    def pack_faces(stage, x, rows, n):
        faces = mm(face, rows.astype(BF16)).astype(BF16)
        for i in range(n):
            part = faces[:, i * 128 : (i + 1) * 128]
            ylo_out[stage, x + i] = part[0:32]
            yhi_out[stage, x + i] = part[32:64]

    def make_x(stage, e):
        xlo_out[stage] = e[:, 4:8].astype(BF16)
        xhi_out[stage] = e[:, TX : TX + 4].astype(BF16)

    def send_x(stage):
        for side in range(2):
            x_copy(stage, side).start()

    def receive_x(stage, e):
        for side in range(2):
            x_copy(stage, side).wait_recv()
        e[:, 0:4] = xlo_in[stage].astype(F32)
        e[:, TX + 4 : TX + 8] = xhi_in[stage].astype(F32)

    def along_xz(e, out, at, k, x, n):
        here = e[k, pl.ds(x + 4, n)]
        hi, lo = split(here.reshape(n * TY, NZ))
        res = mm(jnp.concatenate([hi, lo], axis=1), cz[k])
        total = here + (res[:, 0:128] + res[:, 128:]).reshape(n, TY, NZ)
        v, s1 = viscosity[k], speeds[0, k]
        for m in range(1, 5):
            b, a = time_step * curve_weights[m - 1] * v, time_step * slope_weights[m - 1] * s1
            total = total + (b - a) * e[k, pl.ds(x + 4 + m, n)] + (b + a) * e[k, pl.ds(x + 4 - m, n)]
        out[k, pl.ds(x + at, n)] = total

    def along_y(e, out, at, x):
        hi, lo = split(wide(e, x + 4, 8))
        res = mm(wy[...], jnp.concatenate([hi, lo], axis=0))
        res = res[0:128] + res[128:]
        for n in range(8):
            out[:, x + at + n] = out[:, x + at + n] + res[:, n * 128 : (n + 1) * 128].reshape(V, TY, NZ)

    def from_halo(stage, x, n):
        rhs = jnp.concatenate(
            [jnp.concatenate([ylo_in[stage, x + i], yhi_in[stage, x + i]], axis=0) for i in range(n)], axis=1
        )
        res = mm(wh[...], rhs)
        return res[0:128] + res[128:]

    load.wait()
    make_x(0, e1)

    @pl.loop(0, TX // 8)
    def _(i):
        pack_faces(0, i * 8, wide(e1, i * 8 + 4, 8), 8)

    square = (128, 128)
    turn = (iota(square, 0) - iota(square, 1)) & 127
    turn = jnp.where(turn > 64, turn - 128, turn)
    z_curve, z_slope = curve_of(turn), slope_of(turn)
    y_shape = (TY, 128)
    y_dist = (iota(y_shape, 1) & 15) - iota(y_shape, 0)
    y_var = lax.shift_right_logical(iota(y_shape, 1), 4)
    y_curve = jnp.where(y_dist == 0, time_step * 3.0 * curve_center, curve_of(y_dist))
    y_slope = slope_of(y_dist)
    h_shape = (TY, 64)
    h_col = iota(h_shape, 1)
    h_dist = (h_col & 3) - 4 + lax.shift_right_logical(h_col, 5) * 20 - iota(h_shape, 0)
    h_var = lax.shift_right_logical(h_col, 2) & 7
    h_curve, h_slope = curve_of(h_dist), slope_of(h_dist)

    @pl.loop(0, V)
    def _(k):
        v, s2, s3 = viscosity[k], speeds[1, k], speeds[2, k]
        ch, cl = split(v * z_curve + s3 * z_slope)
        cz[k] = jnp.concatenate(
            [jnp.concatenate([ch, cl], axis=1), jnp.concatenate([ch, jnp.zeros_like(cl)], axis=1)], axis=0
        )
        w = jnp.where(y_var == k, v * y_curve + s2 * y_slope, 0.0)
        for j in range(V):
            w = w + jnp.where((y_var == j) & (y_dist == 0), time_step * reaction[k, j], 0.0)
        hi, lo = split(w)
        at = pl.ds(pl.multiple_of(k * TY, TY), TY)
        at2 = pl.ds(pl.multiple_of(128 + k * TY, TY), TY)
        wy[at, :] = jnp.concatenate([hi, hi], axis=1)
        wy[at2, :] = jnp.concatenate([lo, jnp.zeros_like(lo)], axis=1)
        hi, lo = split(jnp.where(h_var == k, v * h_curve + s2 * h_slope, 0.0))
        wh[at, :] = hi
        wh[at2, :] = lo

    pl.semaphore_wait(barrier, TILES - 1 + ROWS - 1)
    send_x(0)
    for side in range(2):
        y_copy(0, side).start()

    for p in range(TILES):
        count = jnp.int32(0)
        place = [jnp.int32(0)] * MOST
        valid = [jnp.int32(0)] * MOST
        for u in range(UNITS):
            hit = table[gy, 0, u] == p
            for m in range(MOST):
                take = hit & (count == m)
                place[m] = jnp.where(take, UNIT_ORDER.index(u), place[m])
                valid[m] = jnp.where(take, 1, valid[m])
            count = count + hit.astype(jnp.int32)
        for m in range(MOST):
            picks[p, m] = place[m]
            picks[p, MOST + m] = valid[m]

    hi, lo = split(start_ref[...])
    start_t[...] = jnp.zeros((2 * RP, NX), BF16)
    start_t[0:R, :] = hi
    start_t[RP : RP + R, :] = lo

    @pl.loop(0, V, unroll=2)
    def _(k):
        along_xz(e1, e2, 4, k, 8, 16)
        along_xz(e1, e2, 4, k, 24, 16)

    @pl.loop(1, TX // 8 - 1)
    def _(i):
        along_y(e1, e2, 4, i * 8)

    receive_x(0, e1)

    @pl.loop(0, V, unroll=2)
    def _(k):
        along_xz(e1, e2, 4, k, 0, 8)
        along_xz(e1, e2, 4, k, TX - 8, 8)

    for x in (0, TX - 8):
        along_y(e1, e2, 4, x)

    for side in range(2):
        y_copy(0, side).wait_recv()

    def finish_first(x):
        rows = wide(e2, x + 4, 8) + from_halo(0, x, 8)
        for j in range(8):
            e2[:, x + 4 + j] = rows[:, j * 128 : (j + 1) * 128].reshape(V, TY, NZ)
        pack_faces(1, x, rows, 8)

    for x in (0, TX - 8):
        finish_first(x)
    make_x(1, e2)
    send_x(1)

    @pl.loop(1, TX // 8 - 1)
    def _(i):
        finish_first(i * 8)

    for side in range(2):
        y_copy(1, side).start()

    def order_lines(part, c):
        pick = pick_early if part == 0 else pick_late
        at = slice(c * CH, c * CH + CH)

        @pl.loop(0, V // 2, unroll=2)
        def _(i):
            both_k = []
            for k in (i * 2, i * 2 + 1):
                lines = acc[k, at]
                if part == 0:
                    lines = 0.5 * (e1[k, c * CH + 4 : c * CH + CH + 4] + lines)
                    acc[k, at] = lines
                both_k.append(lines.reshape(CH * TY, NZ).astype(BF16))
            got = mm(pick, jnp.concatenate(both_k, axis=1)).astype(BF16)
            for n in range(2):
                for j in range(2):
                    for u in range(4):
                        r = (j * 4 + u) * 16
                        lane = part * 512 + u * 128
                        sbuf[i * 2 + n, j, at, lane : lane + 128] = got[r : r + 16, n * 128 : n * 128 + 128]

    def s_copy(part, n, arrival):
        g, x, peer = tile_at(n, back=arrival)
        source = peer if arrival else me
        lanes = pl.ds(part * 512, 512)
        return pltpu.make_async_remote_copy(
            src_ref=sbuf.at[lax.div(peer, 2), lax.rem(peer, 2), :, lanes],
            dst_ref=srec.at[pl.ds(pl.multiple_of(source * TX, TX), TX), lanes],
            send_sem=s_send.at[part, n], recv_sem=s_recv.at[part, n],
            device_id=(g, x, gy), device_id_type=MESH,
        )

    mine = pl.ds(pl.multiple_of(me * TX, TX), TX)

    def send_lines(part):
        for n in range(15):
            s_copy(part, n, False).start()
        lanes = slice(part * 512, part * 512 + 512)
        srec[mine, lanes] = sbuf[lax.div(me, 2), lax.rem(me, 2), :, lanes]

    def receive_lines(part):
        for n in range(15):
            s_copy(part, n, True).wait_recv()

    def add_product(part):
        lanes = slice(part * 512, part * 512 + 512)
        res = mm(start_t[...], srec[:, lanes])
        hi, lo = split(res[0:RP] + res[RP:])
        right = jnp.concatenate([hi, lo], axis=0)

        @pl.loop(0, NX // 256, unroll=3)
        def _(i):
            at = pl.ds(pl.multiple_of(i * 256, 256), 256)
            got = mm_nt(srec[at, lanes], right)
            got = got[:, 0:RP] + got[:, RP:]
            if part == 0:
                pacc[at, :] = got
            else:
                got = pacc[at, :] + got
                pacc[at, :] = got
                psend[at, :] = got.astype(BF16)

    @pl.loop(0, V, unroll=2)
    def _(k):
        along_xz(e2, acc, 0, k, 8, 16)
        along_xz(e2, acc, 0, k, 24, 16)

    @pl.loop(1, TX // 8 - 1)
    def _(i):
        along_y(e2, acc, 0, i * 8)

    order_lines(0, 1)
    receive_x(1, e2)

    @pl.loop(0, V, unroll=2)
    def _(k):
        along_xz(e2, acc, 0, k, 0, 8)
        along_xz(e2, acc, 0, k, TX - 8, 8)

    for x in (0, TX - 8):
        along_y(e2, acc, 0, x)
    for c in (0, 2):
        order_lines(0, c)
    for side in range(2):
        y_copy(1, side).wait_recv()
    send_lines(0)
    for c in range(CHUNKS):
        for i in range(CH // 8):
            x = c * CH + i * 8
            rows = 0.5 * from_halo(1, x, 8)
            for j in range(8):
                acc[:, x + j] = acc[:, x + j] + rows[:, j * 128 : (j + 1) * 128].reshape(V, TY, NZ)
        order_lines(1, c)

    send_lines(1)
    receive_lines(0)
    add_product(0)
    receive_lines(1)
    add_product(1)

    def p_copy(n, arrival):
        g, x, peer = tile_at(n, back=arrival)
        to, source = (me, peer) if arrival else (peer, me)
        return pltpu.make_async_remote_copy(
            src_ref=psend.at[pl.ds(pl.multiple_of(to * TX, TX), TX)], dst_ref=prec.at[source],
            send_sem=p_send.at[n], recv_sem=p_recv.at[n], device_id=(g, x, gy), device_id_type=MESH,
        )

    for n in range(15):
        p_copy(n, False).start()
    prec[me] = psend[mine, :]
    for n in range(15):
        p_copy(n, True).wait_recv()

    total = prec[0].astype(F32)
    for i in range(1, TILES):
        total = total + prec[i].astype(F32)
    qrec[gy] = total

    def q_copy(d, peer, source):
        return pltpu.make_async_remote_copy(
            src_ref=qrec.at[gy], dst_ref=qrec.at[source],
            send_sem=q_send.at[d], recv_sem=q_recv.at[d], device_id=row(peer), device_id_type=MESH,
        )

    @pl.loop(1, ROWS)
    def _(d):
        q_copy(d, wrap(gy + d, ROWS), gy).start()

    @pl.loop(1, ROWS)
    def _(d):
        q_copy(d, gy, wrap(gy + ROWS - d, ROWS)).wait_recv()

    total = qrec[0]
    for i in range(1, ROWS):
        total = total + qrec[i]
    pfull[mine, :] = total

    def rows_of(i):
        return pl.ds(pl.multiple_of(i * TX, TX), TX)

    def f_copy(n, arrival):
        g, x, peer = tile_at(n, back=arrival)
        at = rows_of(peer if arrival else me)
        return pltpu.make_async_remote_copy(
            src_ref=pfull.at[at], dst_ref=pfull.at[at],
            send_sem=f_send.at[n], recv_sem=f_recv.at[n], device_id=(g, x, gy), device_id_type=MESH,
        )

    def f_pass(n, arrival):
        g, x, peer = tile_at(n, back=True)
        _, x2, partner = tile_at(PARTNER)
        at = rows_of(peer - lax.rem(gx, 2) + lax.rem(x2, 2) if arrival else peer)
        return pltpu.make_async_remote_copy(
            src_ref=pfull.at[at], dst_ref=pfull.at[at],
            send_sem=g_send.at[n], recv_sem=g_recv.at[n], device_id=(grp, x2, gy), device_id_type=MESH,
        )

    for n in SAME_CORE + (PARTNER,):
        f_copy(n, False).start()
    for n in SAME_CORE[1:] + SAME_CORE[:1]:
        f_copy(n, True).wait_recv()
        f_pass(n, False).start()
    f_copy(PARTNER, True).wait_recv()
    for n in SAME_CORE:
        f_pass(n, True).wait_recv()

    product = pfull[...]
    turned = product.T
    prod_t[...] = turned
    norm = jnp.sum(jnp.sum(product * product, axis=0, keepdims=True), axis=1, keepdims=True)
    hi, lo = split(turned)
    inner = mm_nt(hi, hi) + (mm_nt(hi, lo) + mm_nt(lo, hi))
    inner = inner / norm
    ident = (iota(square, 0) == iota(square, 1)).astype(F32)
    chain = None
    for n in range(NEWTON):
        factor = 1.5 * ident - 0.5 * inner
        chain = factor if n == 0 else both(factor, chain)
        if n < NEWTON - 1:
            inner = both(factor, both(inner, factor))
    basis_t = both(chain, prod_t[...]) / jnp.sqrt(norm)
    half = basis_t.astype(BF16)
    for u in range(0, UNITS, 4):
        got = mm(half, srec[:, u * 128 : (u + 4) * 128])[0:R].astype(BF16)
        for i in range(4):
            blocks[u + i] = got[:, i * 128 : (i + 1) * 128]

    @pl.loop(0, TILES)
    def _(p):
        for m in range(MOST):
            got = blocks[picks[p, m]]
            csend[p, m] = jnp.where(picks[p, MOST + m] == 1, got, jnp.zeros_like(got))

    def c_copy(n, arrival):
        g, x, peer = tile_at(n, back=arrival)
        to, source = (me, peer) if arrival else (peer, me)
        return pltpu.make_async_remote_copy(
            src_ref=csend.at[to], dst_ref=crec.at[source],
            send_sem=c_send.at[n], recv_sem=c_recv.at[n], device_id=(g, x, gy), device_id_type=MESH,
        )

    for n in range(15):
        c_copy(n, False).start()
    crec[me] = csend[me]
    for n in range(15):
        c_copy(n, True).wait_recv()

    for stage in range(2):
        for side in range(2):
            x_copy(stage, side).wait_send()
            y_copy(stage, side).wait_send()

    for n in range(15):
        for part in range(2):
            s_copy(part, n, False).wait_send()
        p_copy(n, False).wait_send()
        c_copy(n, False).wait_send()
    for n in SAME_CORE:
        f_copy(n, False).wait_send()
        f_pass(n, False).wait_send()
    f_copy(PARTNER, False).wait_send()

    @pl.loop(1, ROWS)
    def _(d):
        q_copy(d, wrap(gy + d, ROWS), gy).wait_send()


def unpack(final_ref, core_ref, final_out, out_hbm, out, final_sem, store_sem):
    final = pltpu.make_async_copy(final_ref, final_out, final_sem)
    final.start()
    stores = [pltpu.make_async_copy(out.at[m], out_hbm.at[m], store_sem.at[m]) for m in range(MOST)]
    for m in range(MOST):
        for s in range(TILES):
            out[m, :, s, :] = core_ref[s, m].astype(F32)
        stores[m].start()
    final.wait()
    for store in stores:
        store.wait()


def on_device(flow_state, speeds, viscosity, reaction, start_basis, slab_table):
    dma = pltpu.SemaphoreType.DMA
    vmem = pltpu.VMEM
    halo_y = vmem((2, TX, 32, NZ), BF16)
    halo_x = vmem((2, V, 4, TY, NZ), BF16)
    hbm = pl.BlockSpec(memory_space=pl.ANY)
    smem = pl.BlockSpec(memory_space=pltpu.SMEM)
    vm = pl.BlockSpec(memory_space=pltpu.VMEM)
    final_state, cores = pl.pallas_call(
        kernel,
        name="sections_and_core",
        out_shape=(vmem((V, TX, TY, NZ), F32), vmem((TILES, MOST, R, NZ), BF16)),
        in_specs=[hbm, smem, smem, smem, vm, smem],
        out_specs=(vm, vm),
        scratch_shapes=[
            vmem((V, TX + 8, TY, NZ), F32),
            vmem((V, TX + 8, TY, NZ), F32),
            halo_y, halo_y, halo_y, halo_y,
            halo_x, halo_x, halo_x, halo_x,
            vmem((V, 2, TX, UNITS * NZ), BF16),
            vmem((NX, UNITS * NZ), BF16),
            vmem((V, 256, 256), BF16),
            vmem((256, 256), BF16),
            vmem((256, 64), BF16),
            vmem((2 * RP, NX), BF16),
            vmem((NX, RP), F32),
            vmem((NX, RP), BF16),
            vmem((TILES, TX, RP), BF16),
            vmem((ROWS, TX, RP), F32),
            vmem((NX, RP), F32),
            vmem((RP, NX), F32),
            vmem((UNITS, R, NZ), BF16),
            vmem((TILES, MOST, R, NZ), BF16),
            pltpu.SMEM((TILES, 2 * MOST), jnp.int32),
            dma(()),
            dma((2, 2)), dma((2, 2)), dma((2, 2)), dma((2, 2)),
            dma((2, 15)), dma((2, 15)),
            dma((15,)), dma((15,)), dma((ROWS,)), dma((ROWS,)),
            dma((15,)), dma((15,)), dma((15,)), dma((15,)), dma((15,)), dma((15,)),
        ],
        compiler_params=pltpu.CompilerParams(
            collective_id=0, has_side_effects=True, vmem_limit_bytes=60 * 1024 * 1024
        ),
    )(flow_state, speeds, viscosity, reaction, start_basis.T, slab_table.transpose(0, 2, 1))
    final_state, core_slots = pl.pallas_call(
        unpack,
        name="unpack_core",
        out_shape=(
            jax.ShapeDtypeStruct((V, TX, TY, NZ), F32),
            jax.ShapeDtypeStruct((MOST, R, TILES, NZ), F32),
        ),
        in_specs=[vm, vm],
        out_specs=(hbm, hbm),
        scratch_shapes=[
            vmem((MOST, R, TILES, NZ), F32),
            dma(()), dma((MOST,)),
        ],
        compiler_params=pltpu.CompilerParams(vmem_limit_bytes=32 * 1024 * 1024),
    )(final_state, cores)
    return final_state, core_slots.reshape(MOST, R, V, 2, NZ)


def solution(mesh):
    field = P(None, ("grp", "gx"), "gy", None)
    return jax.shard_map(
        on_device,
        mesh=mesh,
        in_specs=(field, P(), P(), P(), P(), P()),
        out_specs=(field, P(("grp", "gx", "gy"), None, None, None, None)),
        check_vma=False,
    )
```

```python
import jax
import jax.numpy as jnp
from jax import lax
from jax.experimental import pallas as pl
from jax.experimental.pallas import tpu as pltpu
from jax.sharding import PartitionSpec as P

V = 8
NX = 768
R = 96
RP = 128
NZ = 128
TX = 48
TY = 16
TILES = 16
ROWS = 8
UNITS = 8
MOST = 2
NEWTON = 5
CH = 16
CHUNKS = TX // CH
PEERS = (
    (2, 1, 0), (1, 0, 0), (3, 0, 0), (0, 1, 0), (2, 1, 1), (1, 0, 1), (3, 0, 1), (0, 1, 1),
    (2, 0, 0), (1, 1, 0), (3, 1, 0), (2, 0, 1), (1, 1, 1), (3, 1, 1), (0, 0, 1),
)
SAME_CORE = tuple(n for n in range(15) if PEERS[n][2] == 0)
PARTNER = 14
EARLY = (2, 3, 4, 5)
LATE = (0, 1, 6, 7)
UNIT_ORDER = EARLY + LATE

slope_weights = (0.8, -0.2, 4.0 / 105.0, -1.0 / 280.0)
curve_weights = (1.6, -0.2, 8.0 / 315.0, -1.0 / 560.0)
curve_center = -205.0 / 72.0
time_step = 0.2

MESH = pl.DeviceIdType.MESH
F32 = jnp.float32
BF16 = jnp.bfloat16
NT = (((1,), (1,)), ((), ()))


def split(x):
    high = x.astype(BF16)
    return high, (x - high.astype(F32)).astype(BF16)


def mm(a, b):
    return jnp.dot(a, b, preferred_element_type=F32)


def mm_nt(a, b):
    return lax.dot_general(a, b, NT, preferred_element_type=F32)


def both(a, b):

    ah, al = split(a)
    bh, bl = split(b)
    left = jnp.concatenate([ah, ah, al], axis=1)
    right = jnp.concatenate([bh, bl, bh], axis=0)
    return mm(left, right)


def iota(shape, dim):
    return lax.broadcasted_iota(jnp.int32, shape, dim)


def curve_of(distance):
    out = jnp.zeros(distance.shape, F32)
    for m in range(1, 5):
        hit = (distance == m) | (distance == -m)
        out = jnp.where(hit, time_step * curve_weights[m - 1], out)
    return out


def slope_of(distance):
    out = jnp.zeros(distance.shape, F32)
    for m in range(1, 5):
        out = jnp.where(distance == m, -time_step * slope_weights[m - 1], out)
        out = jnp.where(distance == -m, time_step * slope_weights[m - 1], out)
    return out


def kernel(
    flow_hbm, speeds, viscosity, reaction, start_ref, table,
    acc, crec,
    e1, e2,
    ylo_out, yhi_out, ylo_in, yhi_in,
    xlo_out, xhi_out, xlo_in, xhi_in,
    sbuf, srec,
    cz, wy, wh,
    start_t, pacc, psend, prec, qrec, pfull, prod_t, blocks, csend,
    picks,
    load_sem,
    y_send, y_recv, x_send, x_recv, s_send, s_recv,
    p_send, p_recv, q_send, q_recv, f_send, f_recv, g_send, g_recv, c_send, c_recv,
):
    grp, gx, gy = (lax.axis_index(a) for a in ("grp", "gx", "gy"))
    me = grp * 4 + gx

    def tile(i):
        return (lax.div(i, 4), lax.rem(i, 4), gy)

    def tile_at(n, back=False):
        dg, dz, dc = PEERS[n]
        g = lax.rem(grp + (4 - dg if back else dg), 4)
        x = lax.rem(lax.div(gx, 2) + dz, 2) * 2 + lax.rem(gx + dc, 2)
        return g, x, g * 4 + x

    def row(i):
        return (grp, gx, i)

    def wrap(i, n):
        return lax.rem(i, n)

    barrier = pltpu.get_barrier_semaphore()

    @pl.loop(1, TILES)
    def _(d):
        pl.semaphore_signal(barrier, inc=1, device_id=tile(wrap(me + d, TILES)), device_id_type=MESH)

    @pl.loop(1, ROWS)
    def _(d):
        pl.semaphore_signal(barrier, inc=1, device_id=row(wrap(gy + d, ROWS)), device_id_type=MESH)

    load = pltpu.make_async_copy(flow_hbm, e1.at[:, 4 : 4 + TX], load_sem)
    load.start()

    f_row, f_col = iota((64, 128), 0), iota((64, 128), 1)
    f_src = (lax.shift_right_logical(f_row, 2) & 7) * 16 + (f_row & 3) + lax.shift_right_logical(f_row, 5) * 12
    face = (f_src == f_col).astype(BF16)

    q_row, q_col = iota((128, 256), 0), iota((128, 256), 1)
    q_unit = lax.shift_right_logical(q_row, 4) & 3
    q_par = lax.shift_right_logical(q_row, 6)
    q_base = (q_row & 15) * 16 + q_par
    pick_early = (q_base + 2 * (q_unit + 2) == q_col).astype(BF16)
    pick_late = (q_base + 2 * jnp.where(q_unit < 2, q_unit, q_unit + 4) == q_col).astype(BF16)

    def y_copy(stage, side):
        out, into = (ylo_out, yhi_in) if side == 0 else (yhi_out, ylo_in)
        peer = row(wrap(gy + (ROWS - 1 if side == 0 else 1), ROWS))
        return pltpu.make_async_remote_copy(
            src_ref=out.at[stage], dst_ref=into.at[stage],
            send_sem=y_send.at[stage, side], recv_sem=y_recv.at[stage, side],
            device_id=peer, device_id_type=MESH,
        )

    def x_copy(stage, side):
        out, into = (xlo_out, xhi_in) if side == 0 else (xhi_out, xlo_in)
        peer = tile(wrap(me + (TILES - 1 if side == 0 else 1), TILES))
        return pltpu.make_async_remote_copy(
            src_ref=out.at[stage], dst_ref=into.at[stage],
            send_sem=x_send.at[stage, side], recv_sem=x_recv.at[stage, side],
            device_id=peer, device_id_type=MESH,
        )

    def wide(ref, x, n):
        return jnp.concatenate([ref[:, x + i].reshape(128, 128) for i in range(n)], axis=1)

    def pack_faces(stage, x, rows, n):
        faces = mm(face, rows.astype(BF16)).astype(BF16)
        for i in range(n):
            part = faces[:, i * 128 : (i + 1) * 128]
            ylo_out[stage, x + i] = part[0:32]
            yhi_out[stage, x + i] = part[32:64]

    def make_x(stage, e):
        xlo_out[stage] = e[:, 4:8].astype(BF16)
        xhi_out[stage] = e[:, TX : TX + 4].astype(BF16)

    def send_x(stage):
        for side in range(2):
            x_copy(stage, side).start()

    def receive_x(stage, e):
        for side in range(2):
            x_copy(stage, side).wait_recv()
        e[:, 0:4] = xlo_in[stage].astype(F32)
        e[:, TX + 4 : TX + 8] = xhi_in[stage].astype(F32)

    def along_xz(e, out, at, k, x, n):
        here = e[k, pl.ds(x + 4, n)]
        hi, lo = split(here.reshape(n * TY, NZ))
        res = mm(jnp.concatenate([hi, lo], axis=1), cz[k])
        total = here + (res[:, 0:128] + res[:, 128:]).reshape(n, TY, NZ)
        v, s1 = viscosity[k], speeds[0, k]
        for m in range(1, 5):
            b, a = time_step * curve_weights[m - 1] * v, time_step * slope_weights[m - 1] * s1
            total = total + (b - a) * e[k, pl.ds(x + 4 + m, n)] + (b + a) * e[k, pl.ds(x + 4 - m, n)]
        out[k, pl.ds(x + at, n)] = total

    def along_y(e, out, at, x):
        hi, lo = split(wide(e, x + 4, 8))
        res = mm(wy[...], jnp.concatenate([hi, lo], axis=0))
        res = res[0:128] + res[128:]
        for n in range(8):
            out[:, x + at + n] = out[:, x + at + n] + res[:, n * 128 : (n + 1) * 128].reshape(V, TY, NZ)

    def from_halo(stage, x, n):
        rhs = jnp.concatenate(
            [jnp.concatenate([ylo_in[stage, x + i], yhi_in[stage, x + i]], axis=0) for i in range(n)], axis=1
        )
        res = mm(wh[...], rhs)
        return res[0:128] + res[128:]

    load.wait()
    make_x(0, e1)

    @pl.loop(0, TX // 8)
    def _(i):
        pack_faces(0, i * 8, wide(e1, i * 8 + 4, 8), 8)

    square = (128, 128)
    turn = (iota(square, 0) - iota(square, 1)) & 127
    turn = jnp.where(turn > 64, turn - 128, turn)
    z_curve, z_slope = curve_of(turn), slope_of(turn)
    y_shape = (TY, 128)
    y_dist = (iota(y_shape, 1) & 15) - iota(y_shape, 0)
    y_var = lax.shift_right_logical(iota(y_shape, 1), 4)
    y_curve = jnp.where(y_dist == 0, time_step * 3.0 * curve_center, curve_of(y_dist))
    y_slope = slope_of(y_dist)
    h_shape = (TY, 64)
    h_col = iota(h_shape, 1)
    h_dist = (h_col & 3) - 4 + lax.shift_right_logical(h_col, 5) * 20 - iota(h_shape, 0)
    h_var = lax.shift_right_logical(h_col, 2) & 7
    h_curve, h_slope = curve_of(h_dist), slope_of(h_dist)

    @pl.loop(0, V)
    def _(k):
        v, s2, s3 = viscosity[k], speeds[1, k], speeds[2, k]
        ch, cl = split(v * z_curve + s3 * z_slope)
        cz[k] = jnp.concatenate(
            [jnp.concatenate([ch, cl], axis=1), jnp.concatenate([ch, jnp.zeros_like(cl)], axis=1)], axis=0
        )
        w = jnp.where(y_var == k, v * y_curve + s2 * y_slope, 0.0)
        for j in range(V):
            w = w + jnp.where((y_var == j) & (y_dist == 0), time_step * reaction[k, j], 0.0)
        hi, lo = split(w)
        at = pl.ds(pl.multiple_of(k * TY, TY), TY)
        at2 = pl.ds(pl.multiple_of(128 + k * TY, TY), TY)
        wy[at, :] = jnp.concatenate([hi, hi], axis=1)
        wy[at2, :] = jnp.concatenate([lo, jnp.zeros_like(lo)], axis=1)
        hi, lo = split(jnp.where(h_var == k, v * h_curve + s2 * h_slope, 0.0))
        wh[at, :] = hi
        wh[at2, :] = lo

    pl.semaphore_wait(barrier, TILES - 1 + ROWS - 1)
    send_x(0)
    for side in range(2):
        y_copy(0, side).start()

    for p in range(TILES):
        count = jnp.int32(0)
        place = [jnp.int32(0)] * MOST
        valid = [jnp.int32(0)] * MOST
        for u in range(UNITS):
            hit = table[gy, 0, u] == p
            for m in range(MOST):
                take = hit & (count == m)
                place[m] = jnp.where(take, UNIT_ORDER.index(u), place[m])
                valid[m] = jnp.where(take, 1, valid[m])
            count = count + hit.astype(jnp.int32)
        for m in range(MOST):
            picks[p, m] = place[m]
            picks[p, MOST + m] = valid[m]

    hi, lo = split(start_ref[...])
    start_t[...] = jnp.zeros((2 * RP, NX), BF16)
    start_t[0:R, :] = hi
    start_t[RP : RP + R, :] = lo

    @pl.loop(0, V, unroll=2)
    def _(k):
        along_xz(e1, e2, 4, k, 8, 16)
        along_xz(e1, e2, 4, k, 24, 16)

    @pl.loop(1, TX // 8 - 1)
    def _(i):
        along_y(e1, e2, 4, i * 8)

    receive_x(0, e1)

    @pl.loop(0, V, unroll=2)
    def _(k):
        along_xz(e1, e2, 4, k, 0, 8)
        along_xz(e1, e2, 4, k, TX - 8, 8)

    for x in (0, TX - 8):
        along_y(e1, e2, 4, x)

    for side in range(2):
        y_copy(0, side).wait_recv()

    def finish_first(x):
        rows = wide(e2, x + 4, 8) + from_halo(0, x, 8)
        for j in range(8):
            e2[:, x + 4 + j] = rows[:, j * 128 : (j + 1) * 128].reshape(V, TY, NZ)
        pack_faces(1, x, rows, 8)

    for x in (0, TX - 8):
        finish_first(x)
    make_x(1, e2)
    send_x(1)

    @pl.loop(1, TX // 8 - 1)
    def _(i):
        finish_first(i * 8)

    for side in range(2):
        y_copy(1, side).start()

    def order_lines(part, c):
        pick = pick_early if part == 0 else pick_late
        at = slice(c * CH, c * CH + CH)

        @pl.loop(0, V // 2, unroll=2)
        def _(i):
            both_k = []
            for k in (i * 2, i * 2 + 1):
                lines = acc[k, at]
                if part == 0:
                    lines = 0.5 * (e1[k, c * CH + 4 : c * CH + CH + 4] + lines)
                    acc[k, at] = lines
                both_k.append(lines.reshape(CH * TY, NZ).astype(BF16))
            got = mm(pick, jnp.concatenate(both_k, axis=1)).astype(BF16)
            for n in range(2):
                for j in range(2):
                    for u in range(4):
                        r = (j * 4 + u) * 16
                        lane = part * 512 + u * 128
                        sbuf[i * 2 + n, j, at, lane : lane + 128] = got[r : r + 16, n * 128 : n * 128 + 128]

    def s_copy(part, n, arrival):
        g, x, peer = tile_at(n, back=arrival)
        source = peer if arrival else me
        lanes = pl.ds(part * 512, 512)
        return pltpu.make_async_remote_copy(
            src_ref=sbuf.at[lax.div(peer, 2), lax.rem(peer, 2), :, lanes],
            dst_ref=srec.at[pl.ds(pl.multiple_of(source * TX, TX), TX), lanes],
            send_sem=s_send.at[part, n], recv_sem=s_recv.at[part, n],
            device_id=(g, x, gy), device_id_type=MESH,
        )

    mine = pl.ds(pl.multiple_of(me * TX, TX), TX)

    def send_lines(part):
        for n in range(15):
            s_copy(part, n, False).start()
        lanes = slice(part * 512, part * 512 + 512)
        srec[mine, lanes] = sbuf[lax.div(me, 2), lax.rem(me, 2), :, lanes]

    def receive_lines(part):
        for n in range(15):
            s_copy(part, n, True).wait_recv()

    def add_product(part):
        lanes = slice(part * 512, part * 512 + 512)
        res = mm(start_t[...], srec[:, lanes])
        hi, lo = split(res[0:RP] + res[RP:])
        right = jnp.concatenate([hi, lo], axis=0)

        @pl.loop(0, NX // 256, unroll=3)
        def _(i):
            at = pl.ds(pl.multiple_of(i * 256, 256), 256)
            got = mm_nt(srec[at, lanes], right)
            got = got[:, 0:RP] + got[:, RP:]
            if part == 0:
                pacc[at, :] = got
            else:
                got = pacc[at, :] + got
                pacc[at, :] = got
                psend[at, :] = got.astype(BF16)

    @pl.loop(0, V, unroll=2)
    def _(k):
        along_xz(e2, acc, 0, k, 8, 16)
        along_xz(e2, acc, 0, k, 24, 16)

    @pl.loop(1, TX // 8 - 1)
    def _(i):
        along_y(e2, acc, 0, i * 8)

    order_lines(0, 1)
    receive_x(1, e2)

    @pl.loop(0, V, unroll=2)
    def _(k):
        along_xz(e2, acc, 0, k, 0, 8)
        along_xz(e2, acc, 0, k, TX - 8, 8)

    for x in (0, TX - 8):
        along_y(e2, acc, 0, x)
    for c in (0, 2):
        order_lines(0, c)
    for side in range(2):
        y_copy(1, side).wait_recv()
    send_lines(0)
    for c in range(CHUNKS):
        for i in range(CH // 8):
            x = c * CH + i * 8
            rows = 0.5 * from_halo(1, x, 8)
            for j in range(8):
                acc[:, x + j] = acc[:, x + j] + rows[:, j * 128 : (j + 1) * 128].reshape(V, TY, NZ)
        order_lines(1, c)

    send_lines(1)
    receive_lines(0)
    add_product(0)
    receive_lines(1)
    add_product(1)

    def p_copy(n, arrival):
        g, x, peer = tile_at(n, back=arrival)
        to, source = (me, peer) if arrival else (peer, me)
        return pltpu.make_async_remote_copy(
            src_ref=psend.at[pl.ds(pl.multiple_of(to * TX, TX), TX)], dst_ref=prec.at[source],
            send_sem=p_send.at[n], recv_sem=p_recv.at[n], device_id=(g, x, gy), device_id_type=MESH,
        )

    for n in range(15):
        p_copy(n, False).start()
    prec[me] = psend[mine, :]
    for n in range(15):
        p_copy(n, True).wait_recv()

    total = prec[0].astype(F32)
    for i in range(1, TILES):
        total = total + prec[i].astype(F32)
    qrec[gy] = total

    def q_copy(d, peer, source):
        return pltpu.make_async_remote_copy(
            src_ref=qrec.at[gy], dst_ref=qrec.at[source],
            send_sem=q_send.at[d], recv_sem=q_recv.at[d], device_id=row(peer), device_id_type=MESH,
        )

    @pl.loop(1, ROWS)
    def _(d):
        q_copy(d, wrap(gy + d, ROWS), gy).start()

    @pl.loop(1, ROWS)
    def _(d):
        q_copy(d, gy, wrap(gy + ROWS - d, ROWS)).wait_recv()

    total = qrec[0]
    for i in range(1, ROWS):
        total = total + qrec[i]
    pfull[mine, :] = total

    def rows_of(i):
        return pl.ds(pl.multiple_of(i * TX, TX), TX)

    def f_copy(n, arrival):
        g, x, peer = tile_at(n, back=arrival)
        at = rows_of(peer if arrival else me)
        return pltpu.make_async_remote_copy(
            src_ref=pfull.at[at], dst_ref=pfull.at[at],
            send_sem=f_send.at[n], recv_sem=f_recv.at[n], device_id=(g, x, gy), device_id_type=MESH,
        )

    def f_pass(n, arrival):
        g, x, peer = tile_at(n, back=True)
        _, x2, partner = tile_at(PARTNER)
        at = rows_of(peer - lax.rem(gx, 2) + lax.rem(x2, 2) if arrival else peer)
        return pltpu.make_async_remote_copy(
            src_ref=pfull.at[at], dst_ref=pfull.at[at],
            send_sem=g_send.at[n], recv_sem=g_recv.at[n], device_id=(grp, x2, gy), device_id_type=MESH,
        )

    for n in SAME_CORE + (PARTNER,):
        f_copy(n, False).start()
    for n in SAME_CORE[1:] + SAME_CORE[:1]:
        f_copy(n, True).wait_recv()
        f_pass(n, False).start()
    f_copy(PARTNER, True).wait_recv()
    for n in SAME_CORE:
        f_pass(n, True).wait_recv()

    product = pfull[...]
    turned = product.T
    prod_t[...] = turned
    norm = jnp.sum(jnp.sum(product * product, axis=0, keepdims=True), axis=1, keepdims=True)
    hi, lo = split(turned)
    inner = mm_nt(hi, hi) + (mm_nt(hi, lo) + mm_nt(lo, hi))
    inner = inner / norm
    ident = (iota(square, 0) == iota(square, 1)).astype(F32)
    chain = None
    for n in range(NEWTON):
        factor = 1.5 * ident - 0.5 * inner
        chain = factor if n == 0 else both(factor, chain)
        if n < NEWTON - 1:
            inner = both(factor, both(inner, factor))
    basis_t = both(chain, prod_t[...]) / jnp.sqrt(norm)
    half = basis_t.astype(BF16)
    for u in range(0, UNITS, 4):
        got = mm(half, srec[:, u * 128 : (u + 4) * 128])[0:R].astype(BF16)
        for i in range(4):
            blocks[u + i] = got[:, i * 128 : (i + 1) * 128]

    def pick_blocks(p, out, at):
        for m in range(MOST):
            got = blocks[picks[p, m]]
            out[at, m] = jnp.where(picks[p, MOST + m] == 1, got, jnp.zeros_like(got))

    def c_copy(n, arrival):
        g, x, peer = tile_at(n, back=arrival)
        to, source = (me, peer) if arrival else (peer, me)
        return pltpu.make_async_remote_copy(
            src_ref=csend.at[to], dst_ref=crec.at[source],
            send_sem=c_send.at[n], recv_sem=c_recv.at[n], device_id=(g, x, gy), device_id_type=MESH,
        )

    for n in range(15):
        peer = tile_at(n)[2]
        pick_blocks(peer, csend, peer)
        c_copy(n, False).start()
    pick_blocks(me, crec, me)
    for n in range(15):
        c_copy(n, True).wait_recv()

    for stage in range(2):
        for side in range(2):
            x_copy(stage, side).wait_send()
            y_copy(stage, side).wait_send()

    for n in range(15):
        for part in range(2):
            s_copy(part, n, False).wait_send()
        p_copy(n, False).wait_send()
        c_copy(n, False).wait_send()
    for n in SAME_CORE:
        f_copy(n, False).wait_send()
        f_pass(n, False).wait_send()
    f_copy(PARTNER, False).wait_send()

    @pl.loop(1, ROWS)
    def _(d):
        q_copy(d, wrap(gy + d, ROWS), gy).wait_send()


def unpack(final_ref, core_ref, final_out, out_hbm, out, final_sem, store_sem):
    final = pltpu.make_async_copy(final_ref, final_out, final_sem)
    final.start()
    stores = [pltpu.make_async_copy(out.at[m], out_hbm.at[m], store_sem.at[m]) for m in range(MOST)]
    for m in range(MOST):
        for s in range(TILES):
            out[m, :, s, :] = core_ref[s, m].astype(F32)
        stores[m].start()
    final.wait()
    for store in stores:
        store.wait()


def on_device(flow_state, speeds, viscosity, reaction, start_basis, slab_table):
    dma = pltpu.SemaphoreType.DMA
    vmem = pltpu.VMEM
    halo_y = vmem((2, TX, 32, NZ), BF16)
    halo_x = vmem((2, V, 4, TY, NZ), BF16)
    hbm = pl.BlockSpec(memory_space=pl.ANY)
    smem = pl.BlockSpec(memory_space=pltpu.SMEM)
    vm = pl.BlockSpec(memory_space=pltpu.VMEM)
    final_state, cores = pl.pallas_call(
        kernel,
        name="sections_and_core",
        out_shape=(vmem((V, TX, TY, NZ), F32), vmem((TILES, MOST, R, NZ), BF16)),
        in_specs=[hbm, smem, smem, smem, vm, smem],
        out_specs=(vm, vm),
        scratch_shapes=[
            vmem((V, TX + 8, TY, NZ), F32),
            vmem((V, TX + 8, TY, NZ), F32),
            halo_y, halo_y, halo_y, halo_y,
            halo_x, halo_x, halo_x, halo_x,
            vmem((V, 2, TX, UNITS * NZ), BF16),
            vmem((NX, UNITS * NZ), BF16),
            vmem((V, 256, 256), BF16),
            vmem((256, 256), BF16),
            vmem((256, 64), BF16),
            vmem((2 * RP, NX), BF16),
            vmem((NX, RP), F32),
            vmem((NX, RP), BF16),
            vmem((TILES, TX, RP), BF16),
            vmem((ROWS, TX, RP), F32),
            vmem((NX, RP), F32),
            vmem((RP, NX), F32),
            vmem((UNITS, R, NZ), BF16),
            vmem((TILES, MOST, R, NZ), BF16),
            pltpu.SMEM((TILES, 2 * MOST), jnp.int32),
            dma(()),
            dma((2, 2)), dma((2, 2)), dma((2, 2)), dma((2, 2)),
            dma((2, 15)), dma((2, 15)),
            dma((15,)), dma((15,)), dma((ROWS,)), dma((ROWS,)),
            dma((15,)), dma((15,)), dma((15,)), dma((15,)), dma((15,)), dma((15,)),
        ],
        compiler_params=pltpu.CompilerParams(
            collective_id=0, has_side_effects=True, vmem_limit_bytes=60 * 1024 * 1024
        ),
    )(flow_state, speeds, viscosity, reaction, start_basis.T, slab_table.transpose(0, 2, 1))
    final_state, core_slots = pl.pallas_call(
        unpack,
        name="unpack_core",
        out_shape=(
            jax.ShapeDtypeStruct((V, TX, TY, NZ), F32),
            jax.ShapeDtypeStruct((MOST, R, TILES, NZ), F32),
        ),
        in_specs=[vm, vm],
        out_specs=(hbm, hbm),
        scratch_shapes=[
            vmem((MOST, R, TILES, NZ), F32),
            dma(()), dma((MOST,)),
        ],
        compiler_params=pltpu.CompilerParams(vmem_limit_bytes=32 * 1024 * 1024),
    )(final_state, cores)
    return final_state, core_slots.reshape(MOST, R, V, 2, NZ)


def solution(mesh):
    field = P(None, ("grp", "gx"), "gy", None)
    return jax.shard_map(
        on_device,
        mesh=mesh,
        in_specs=(field, P(), P(), P(), P(), P()),
        out_specs=(field, P(("grp", "gx", "gy"), None, None, None, None)),
        check_vma=False,
    )
```
